512 devices in a mesh: learn: 32 (over z, y_lo, core), roll: 16 (over y_hi, x).
Axes of the slice: x: 4, y: 8 (y_hi: 4, y_lo: 2; y = y_hi * 2 + y_lo), z: 8, core: 2. Of those that a mesh axis runs over, the one named last changes fastest.
Arguments:
- frozen_weight: bfloat16 [8192, 28672], P('roll', 'learn'), may hold values from -0.00048828125 to 0.00048828125
- projection_inputs: bfloat16 [20480, 28672], P('learn', 'roll'), may hold values from -6 to 6
- output_gradients: bfloat16 [20480, 8192], P('learn', 'roll'), may hold values from -6 to 6
- adapter_down_factor: float32 [128, 28672], P('learn', 'roll'), may hold values from -0.01953125 to 0.01953125
- down_first_moment: float32 [128, 28672], P('learn', 'roll'), may hold values from -0.5 to 0.5
- down_second_moment: float32 [128, 28672], P('learn', 'roll'), may hold values from 0.0006 to 0.01
- adapter_up_factor: float32 [128, 8192], P('learn', 'roll'), may hold values from -0.01171875 to 0.01171875
- up_first_moment: float32 [128, 8192], P('learn', 'roll'), may hold values from -1.5 to 1.5
- up_second_moment: float32 [128, 8192], P('learn', 'roll'), may hold values from 0.006 to 0.1
Outputs:
- weight_with_adapter: bfloat16 [8192, 28672], P('roll', 'learn')
- down_factor_updated: float32 [128, 28672], P('learn', 'roll')
- down_first_updated: float32 [128, 28672], P('learn', 'roll')
- down_second_updated: float32 [128, 28672], P('learn', 'roll')
- up_factor_updated: float32 [128, 8192], P('learn', 'roll')
- up_first_updated: float32 [128, 8192], P('learn', 'roll')
- up_second_updated: float32 [128, 8192], P('learn', 'roll')
The draws below stay inside these ranges and needn't reach their ends.
All inputs are finite; a program needn't handle non-finite values.
Results may differ from the reference program's by a relative error of at most 0.018.
Values may be sent and summed in bfloat16 or wider, within the bound.
A program may use at most 64 MiB of HBM per device.

```python
import math
import jax
import jax.numpy as jnp

MODEL_WIDTH = 8192
HIDDEN_WIDTH = 28672
ADAPTER_RANK = 128
STEP = 20
TOKENS = 20480


def block_scale(own_key, extent, pieces, low, largest):
    gain, own = 1.0, jax.random.fold_in(own_key, 6)
    for dim, shards_of in pieces:
        draws = jnp.exp(jax.random.uniform(jax.random.fold_in(own, dim), (shards_of,), jnp.float32, low / len(pieces), largest / len(pieces)))
        gain = gain * jnp.repeat(draws, extent[dim] // shards_of).reshape([-1 if axis == dim else 1 for axis in range(len(extent))])
    return gain


def centred(rng, extent, width, bound, cuts=(), held_as=jnp.bfloat16):
    loudness = block_scale(rng, extent, cuts, -0.22, 0.18) if cuts else 1.0
    drawn = jax.random.normal(rng, extent, jnp.float32) * width * loudness
    return jnp.minimum(jnp.maximum(drawn, -bound), bound).astype(held_as)


def setup_inputs(seed: int = 0) -> dict:
    arg_keys = jax.random.split(jax.random.key(seed), 10)
    frozen_weight = centred(arg_keys[0], (MODEL_WIDTH, HIDDEN_WIDTH), (96 * HIDDEN_WIDTH * MODEL_WIDTH // ADAPTER_RANK) ** -0.5, 0.00048828125, ((0, 16), (1, 32)))
    projection_inputs = centred(arg_keys[1], (TOKENS, HIDDEN_WIDTH), 1.0, 6.0, ((0, 32), (1, 16)))
    output_gradients = centred(arg_keys[2], (TOKENS, MODEL_WIDTH), 1.0, 6.0, ((0, 32), (1, 16)))
    adapter_down_factor = centred(arg_keys[3], (ADAPTER_RANK, HIDDEN_WIDTH), (3 * HIDDEN_WIDTH) ** -0.5, 0.01953125, ((0, 32), (1, 16)), jnp.float32)
    down_first_moment = centred(arg_keys[4], (ADAPTER_RANK, HIDDEN_WIDTH), 0.08, 0.5, ((0, 32), (1, 16)), jnp.float32)
    down_second_moment = jnp.clip(jnp.exp(math.log(0.01) - 2.81341065 * jax.random.uniform(arg_keys[5], (ADAPTER_RANK, HIDDEN_WIDTH), jnp.float32) ** block_scale(arg_keys[5], (ADAPTER_RANK, HIDDEN_WIDTH), ((0, 32), (1, 16)), -0.2, 0.2)), 0.0006, 0.01)
    adapter_up_factor = centred(arg_keys[6], (ADAPTER_RANK, MODEL_WIDTH), (32 * MODEL_WIDTH) ** -0.5, 0.01171875, ((0, 32), (1, 16)), jnp.float32)
    up_first_moment = centred(arg_keys[7], (ADAPTER_RANK, MODEL_WIDTH), 0.25, 1.5, ((0, 32), (1, 16)), jnp.float32)
    up_second_moment = jnp.clip(jnp.exp(math.log(0.1) - 2.8134107 * jax.random.uniform(arg_keys[8], (ADAPTER_RANK, MODEL_WIDTH), jnp.float32) ** block_scale(arg_keys[8], (ADAPTER_RANK, MODEL_WIDTH), ((0, 32), (1, 16)), -0.2, 0.2)), 0.006, 0.1)
    return dict(frozen_weight=frozen_weight, projection_inputs=projection_inputs, output_gradients=output_gradients, adapter_down_factor=adapter_down_factor, down_first_moment=down_first_moment, down_second_moment=down_second_moment, adapter_up_factor=adapter_up_factor, up_first_moment=up_first_moment, up_second_moment=up_second_moment)


adapter_scale = 2.0
learning_rate = 0.001
beta_one = 0.9
beta_two = 0.999
epsilon = 1e-08
weight_decay = 0.01

def decoupled_adam_update(weights, moment_one, moment_two, gradient):
    one_next = beta_one * moment_one + (1.0 - beta_one) * gradient
    two_next = beta_two * moment_two + (1.0 - beta_two) * gradient * gradient
    corr_one = 1.0 - beta_one ** STEP
    corr_two = 1.0 - beta_two ** STEP
    update = one_next / corr_one / (jnp.sqrt(two_next / corr_two) + epsilon)
    return (weights - learning_rate * (update + weight_decay * weights), one_next, two_next)

def reference(frozen_weight, projection_inputs, output_gradients, adapter_down_factor, down_first_moment, down_second_moment, adapter_up_factor, up_first_moment, up_second_moment):
    down_present = adapter_down_factor.astype(jnp.bfloat16)
    up_present = adapter_up_factor.astype(jnp.bfloat16)
    hidden_low_rank = jnp.dot(projection_inputs, down_present.T, preferred_element_type=jnp.float32).astype(jnp.bfloat16)
    backward_low_rank = (adapter_scale * jnp.dot(output_gradients, up_present.T, preferred_element_type=jnp.float32)).astype(jnp.bfloat16)
    normalizer_scale = 1.0 / math.sqrt(TOKENS)
    down_gradient = normalizer_scale * jnp.dot(backward_low_rank.T, projection_inputs, preferred_element_type=jnp.float32)
    up_gradient = adapter_scale * normalizer_scale * jnp.dot(hidden_low_rank.T, output_gradients, preferred_element_type=jnp.float32)
    down_factor_updated, down_first_updated, down_second_updated = decoupled_adam_update(adapter_down_factor, down_first_moment, down_second_moment, down_gradient)
    up_factor_updated, up_first_updated, up_second_updated = decoupled_adam_update(adapter_up_factor, up_first_moment, up_second_moment, up_gradient)
    adapter_product = jnp.dot(up_factor_updated.astype(jnp.bfloat16).T, down_factor_updated.astype(jnp.bfloat16), preferred_element_type=jnp.float32)
    weight_with_adapter = (frozen_weight.astype(jnp.float32) + adapter_scale * adapter_product).astype(jnp.bfloat16)
    return (weight_with_adapter, down_factor_updated, down_first_updated, down_second_updated, up_factor_updated, up_first_updated, up_second_updated)
```

```python
import math

import jax
import jax.numpy as jnp
from jax import lax
from jax.experimental import pallas as pl
from jax.experimental.pallas import tpu as pltpu
from jax.sharding import PartitionSpec as P

MESH = pl.DeviceIdType.MESH
BF16, F32 = jnp.bfloat16, jnp.float32

LEARN, ROLL, NZ, NX, NH = 32, 16, 8, 4, 4
RANK, TOKENS, OWN = 128, 20480, 4
ROWS, HID, OUT, WCOLS = 640, 1792, 512, 896
PART = ROWS // NX
TD, TU, TW = HID // 128, OUT // 128, WCOLS // 128
PD, PU, PW = 64, 16, 32

STEP = 20
adapter_scale = 2.0
learning_rate = 0.001
beta_one = 0.9
beta_two = 0.999
epsilon = 1e-08
weight_decay = 0.01


def adam(weights, moment_one, moment_two, gradient):
    one_next = beta_one * moment_one + (1.0 - beta_one) * gradient
    two_next = beta_two * moment_two + (1.0 - beta_two) * gradient * gradient
    corr_one = 1.0 - beta_one**STEP
    corr_two = 1.0 - beta_two**STEP
    update = one_next / corr_one / (jnp.sqrt(two_next / corr_two) + epsilon)
    return weights - learning_rate * (update + weight_decay * weights), one_next, two_next


def onehot(rows, cols, column_of_row):
    row = lax.broadcasted_iota(jnp.int32, (rows, cols), 0)
    col = lax.broadcasted_iota(jnp.int32, (rows, cols), 1)
    return jnp.where(column_of_row(row) == col, 1.0, 0.0).astype(BF16)


def dot(a, b, ca, cb):
    return lax.dot_general(a, b, (((ca,), (cb,)), ((), ())), preferred_element_type=F32)


def pack(value, tiles, rows):
    parts = [value[:, 128 * t : 128 * t + 128] for t in range(tiles)]
    if rows > OWN * tiles:
        parts.append(jnp.zeros((rows - OWN * tiles, 128), value.dtype))
    return jnp.concatenate(parts, axis=0).astype(BF16)


def unpack(value, tiles):
    return jnp.concatenate([value[OWN * t : OWN * t + OWN] for t in range(tiles)], axis=1)


def kernel(
    w_hbm, x_hbm, g_hbm, dp_hbm, dm_hbm, dv_hbm, up_hbm, um_hbm, uv_hbm,
    wo_hbm, dpo_hbm, dmo_hbm, dvo_hbm, upo_hbm, umo_hbm, uvo_hbm,
    w_v, x_v, g_v, dp_v, dm_v, dv_v, up_v, um_v, uv_v,
    wo_v, dpo_v, dmo_v, dvo_v, upo_v, umo_v, uvo_v,
    ubuf, dbuf, umat, dmat, pu, pd, pdt, put, pw,
    bpart, bx, bh, blow, hpart, hx, hh, hlow,
    gpack, gcore, gsum, gz, upack, ured, unew, fsend, fbuf, dnew,
    load_sem, store_sem, send_sem, recv_sem,
):
    l = lax.axis_index("learn")
    r = lax.axis_index("roll")
    z, zy, q, core = l // 4, l // 2, l % 4, l % 2
    yhi, x = r // 4, r % 4
    core_peer = (l + 1 - 2 * core, r)
    ylo_peer = (l + 2 - 4 * (q // 2), r)

    loads = []
    for k, (src, dst) in enumerate(
        [(up_hbm, up_v), (dp_hbm, dp_v), (g_hbm, g_v), (x_hbm, x_v), (dm_hbm, dm_v), (dv_hbm, dv_v),
         (um_hbm, um_v), (uv_hbm, uv_v), (w_hbm, w_v)]
    ):
        copy = pltpu.make_async_copy(src, dst, load_sem.at[k])
        copy.start()
        loads.append(copy)
    load_up, load_dp, load_g, load_x, load_dm, load_dv, load_um, load_uv, load_w = loads

    barrier = pltpu.get_barrier_semaphore()

    def greet(to):
        pl.semaphore_signal(barrier, inc=1, device_id=to, device_id_type=MESH)

    for k in range(1, LEARN):
        greet(((l + k) % LEARN, r))
    for k in range(1, 4):
        greet((l, yhi * 4 + (x + k) % 4))
        greet((l, ((yhi + k) % 4) * 4 + x))
    source_roll = l // 2
    for k in range(1, LEARN):
        greet(((l + k) % LEARN, source_roll))
    at_home = r == source_roll

    greet((l, source_roll))

    load_up.wait()
    load_dp.wait()
    ubuf[l] = pack(up_v[...], TU, PU)
    dbuf[q, z] = pack(dp_v[...], TD, PD)
    pl.semaphore_wait(barrier, LEARN - 1 + 6 + LEARN)

    def rcopy(src, dst, k, to):
        return pltpu.make_async_remote_copy(
            src_ref=src, dst_ref=dst, send_sem=send_sem.at[k], recv_sem=recv_sem.at[k],
            device_id=to, device_id_type=MESH,
        )

    def drain(ref, sem):
        pltpu.make_async_copy(ref, ref, sem).wait()

    def learn_all(src_of, dst, k):
        def send(j, c):
            to = (l + j) % LEARN
            rcopy(src_of(to), dst.at[l], k, (to, r)).start()
            return c

        lax.fori_loop(1, LEARN, send, 0)

    def x_to(j):
        return yhi * 4 + (x + j) % 4

    def h_to(j):
        return ((yhi + j) % 4) * 4 + x

    learn_all(lambda to: ubuf.at[l], ubuf, 0)
    for j in range(1, NZ):
        rcopy(dbuf.at[q, z], dbuf.at[q, z], 1, (((z + j) % NZ) * 4 + q, r)).start()

    pu[...] = onehot(512, 512, lambda a: ((a & 127) >> 2) * 16 + (a >> 7) * 4 + (a & 3))
    pd[...] = onehot(448, 512, lambda a: ((a & 31) >> 2) * 64 + (a >> 5) * 4 + (a & 3))
    pdt[...] = onehot(
        512, 448,
        lambda a: jnp.where(
            (a & 63) < 56,
            ((a & 63) >> 2) * 32 + ((a >> 6) & 3) * 8 + (a >> 8) * 4 + (a & 3),
            -1,
        ),
    )
    put[...] = onehot(
        512, 512,
        lambda a: ((a & 15) >> 2) * 128 + ((a >> 4) & 3) * 32 + (a >> 6) * 4 + (a & 3),
    )
    pw[...] = onehot(448, 512, lambda a: ((a & 63) >> 2) * 32 + (a >> 6) * 4 + (a & 3))

    drain(ubuf.at[pl.ds(0, LEARN - 1)], recv_sem.at[0])
    spread = dot(pu[...], ubuf[...].reshape(512, 128), 1, 0).astype(BF16)
    for t in range(TU):
        umat[:, 128 * t : 128 * t + 128] = spread[128 * t : 128 * t + 128]
    load_g.wait()
    bpart[...] = dot(g_v[...], umat[...], 1, 1).astype(BF16).reshape(NX, PART, 128)
    for j in range(1, 4):
        rcopy(bpart.at[(x + j) % 4], bx.at[x], 2, (l, x_to(j))).start()
    bx[x] = bpart[x]

    drain(dbuf.at[0, pl.ds(0, NZ - 1)], recv_sem.at[1])
    rcopy(dbuf.at[q], dbuf.at[q], 3, core_peer).start()
    rcopy(dbuf.at[q], dbuf.at[q], 4, ylo_peer).start()

    def sum_four(buf):
        v = buf[...].astype(F32)
        return (v[0] + v[1]) + (v[2] + v[3])

    drain(bx.at[pl.ds(0, 3)], recv_sem.at[2])
    bh[yhi] = sum_four(bx).astype(BF16)
    for j in range(1, 4):
        rcopy(bh.at[yhi], bh.at[yhi], 5, (l, h_to(j))).start()

    drain(dbuf.at[0], recv_sem.at[4])
    q_other = (q + 2) % 4
    rcopy(dbuf.at[q_other], dbuf.at[q_other], 6, core_peer).start()
    drain(dbuf.at[0], recv_sem.at[3])
    drain(dbuf.at[0], recv_sem.at[6])
    for k in range(4):
        spread = dot(pd[...], dbuf[k].reshape(512, 128), 1, 0).astype(BF16)
        for t in range(TD):
            dmat[32 * k : 32 * k + 32, 128 * t : 128 * t + 128] = spread[32 * t : 32 * t + 32]
    load_x.wait()
    hpart[...] = dot(x_v[...], dmat[...], 1, 1).astype(BF16).reshape(NX, PART, 128)
    for j in range(1, 4):
        rcopy(hpart.at[(x + j) % 4], hx.at[x], 7, (l, x_to(j))).start()
    hx[x] = hpart[x]

    drain(bh.at[pl.ds(0, 3)], recv_sem.at[5])
    blow[x] = (adapter_scale * sum_four(bh)).astype(BF16)
    for j in range(1, 4):
        rcopy(blow.at[x], blow.at[x], 8, (l, x_to(j))).start()

    drain(hx.at[pl.ds(0, 3)], recv_sem.at[7])
    hh[yhi] = sum_four(hx).astype(BF16)
    for j in range(1, 4):
        rcopy(hh.at[yhi], hh.at[yhi], 9, (l, h_to(j))).start()

    normalizer_scale = 1.0 / math.sqrt(TOKENS)
    drain(blow.at[pl.ds(0, 3)], recv_sem.at[8])
    grad = (normalizer_scale * dot(blow[...].reshape(ROWS, 128), x_v[...], 0, 0)).astype(BF16)
    for k in range(4):
        stack = jnp.concatenate(
            [grad[32 * k : 32 * k + 32, 128 * t : 128 * t + 128] for t in range(TD)], axis=0
        )
        packed = dot(pdt[...], stack, 1, 0).astype(BF16)
        gpack[0, 4 * k : 4 * k + 4] = packed[:256].reshape(4, PD, 128)
        gpack[1, 4 * k : 4 * k + 4] = packed[256:].reshape(4, PD, 128)
    rcopy(gpack.at[1 - core], gcore, 10, core_peer).start()

    drain(hh.at[pl.ds(0, 3)], recv_sem.at[9])
    hlow[x] = sum_four(hh).astype(BF16)
    for j in range(1, 4):
        rcopy(hlow.at[x], hlow.at[x], 11, (l, x_to(j))).start()

    drain(gcore, recv_sem.at[10])
    gsum[...] = (gpack[core].astype(F32) + gcore[...].astype(F32)).astype(BF16)

    def send_gsum(j, c):
        to = (zy + j) % 16
        rcopy(gsum.at[to], gz.at[zy], 12, (to * 2 + core, r)).start()
        return c

    lax.fori_loop(1, 16, send_gsum, 0)
    gz[zy] = gsum[zy]

    drain(hlow.at[pl.ds(0, 3)], recv_sem.at[11])
    gradu = (adapter_scale * normalizer_scale) * dot(hlow[...].reshape(ROWS, 128), g_v[...], 0, 0)
    gradu = gradu.astype(BF16)
    stack = jnp.concatenate([gradu[:, 128 * t : 128 * t + 128] for t in range(TU)], axis=0)
    upack[...] = dot(put[...], stack, 1, 0).astype(BF16).reshape(LEARN, PU, 128)
    learn_all(lambda to: upack.at[to], ured, 13)
    ured[l] = upack[l]

    stores = []

    def store(k, src, dst):
        copy = pltpu.make_async_copy(src, dst, store_sem.at[k])
        copy.start()
        stores.append(copy)

    for copy in (load_dm, load_dv, load_um, load_uv, load_w):
        copy.wait()
    drain(gz.at[pl.ds(0, 15)], recv_sem.at[12])
    new_p, new_m, new_v = adam(
        dp_v[...], dm_v[...], dv_v[...], unpack(jnp.sum(gz[...].astype(F32), axis=0), TD)
    )
    fsend[0] = pack(new_p[:, :WCOLS], TW, PW)
    fsend[1] = pack(new_p[:, WCOLS:], TW, PW)

    def to_shard(k):
        return 2 * r + k // 16, k % 16

    def send_shard(k, c):
        to_l, to_r = to_shard(k)
        own = jnp.logical_and(to_l == l, to_r == r)

        @pl.when(jnp.logical_not(own))
        def _():
            rcopy(fsend.at[k // 16], fbuf.at[l], 14, (to_l, to_r)).start()

        @pl.when(own)
        def _():
            pltpu.make_async_copy(fsend.at[k // 16], fbuf.at[l], recv_sem.at[14]).start()

        return c

    lax.fori_loop(0, 32, send_shard, 0)
    dpo_v[...] = new_p
    dmo_v[...] = new_m
    dvo_v[...] = new_v
    store(0, dpo_v, dpo_hbm)
    store(1, dmo_v, dmo_hbm)
    store(2, dvo_v, dvo_hbm)

    drain(ured.at[pl.ds(0, LEARN - 1)], recv_sem.at[13])
    new_p, new_m, new_v = adam(
        up_v[...], um_v[...], uv_v[...], unpack(jnp.sum(ured[...].astype(F32), axis=0), TU)
    )
    unew[l] = pack(new_p, TU, PU)
    learn_all(lambda to: unew.at[l], unew, 15)
    upo_v[...] = new_p
    umo_v[...] = new_m
    uvo_v[...] = new_v
    store(3, upo_v, upo_hbm)
    store(4, umo_v, umo_hbm)
    store(5, uvo_v, uvo_hbm)

    drain(fbuf, recv_sem.at[14])
    for k in range(2):
        spread = dot(pw[...], fbuf[16 * k : 16 * k + 16].reshape(512, 128), 1, 0).astype(BF16)
        for t in range(TW):
            dnew[64 * k : 64 * k + 64, 128 * t : 128 * t + 128] = spread[64 * t : 64 * t + 64]
    drain(unew.at[pl.ds(0, LEARN - 1)], recv_sem.at[15])
    spread = dot(pu[...], unew[...].reshape(512, 128), 1, 0).astype(BF16)
    for t in range(TU):
        umat[:, 128 * t : 128 * t + 128] = spread[128 * t : 128 * t + 128]
    product = dot(umat[...], dnew[...], 0, 0)
    wo_v[...] = (w_v[...].astype(F32) + adapter_scale * product).astype(BF16)
    store(6, wo_v, wo_hbm)

    drain(ubuf.at[pl.ds(0, LEARN - 1)], send_sem.at[0])
    drain(dbuf.at[0, pl.ds(0, NZ - 1)], send_sem.at[1])
    for k in (3, 4, 6):
        drain(dbuf.at[0], send_sem.at[k])
    for k in (2, 5, 7, 8, 9, 11):
        drain(bx.at[pl.ds(0, 3)], send_sem.at[k])
    drain(gcore, send_sem.at[10])
    drain(gz.at[pl.ds(0, 15)], send_sem.at[12])
    drain(ured.at[pl.ds(0, LEARN - 1)], send_sem.at[13])
    drain(fbuf.at[pl.ds(0, LEARN - 1)], send_sem.at[14])

    @pl.when(jnp.logical_not(at_home))
    def _():
        drain(fbuf.at[0], send_sem.at[14])

    drain(unew.at[pl.ds(0, LEARN - 1)], send_sem.at[15])
    for copy in stores:
        copy.wait()


def per_device(*args):
    down, up = (OWN, HID), (OWN, OUT)
    small = [down, down, down, up, up, up]
    any_spec = pl.BlockSpec(memory_space=pl.ANY)

    def b(*shape):
        return pltpu.VMEM(shape, BF16)

    low = [b(NX, PART, 128) for _ in range(4)]
    return tuple(pl.pallas_call(
        kernel,
        out_shape=[jax.ShapeDtypeStruct((OUT, WCOLS), BF16)]
        + [jax.ShapeDtypeStruct(s, F32) for s in small],
        in_specs=[any_spec] * 9,
        out_specs=[any_spec] * 7,
        scratch_shapes=[b(OUT, WCOLS), b(ROWS, HID), b(ROWS, OUT)]
        + [pltpu.VMEM(s, F32) for s in small]
        + [b(OUT, WCOLS)]
        + [pltpu.VMEM(s, F32) for s in small]
        + [b(LEARN, PU, 128), b(4, NZ, PD, 128), b(RANK, OUT), b(RANK, HID)]
        + [b(512, 512), b(448, 512), b(512, 448), b(512, 512), b(448, 512)]
        + low
        + low
        + [b(2, 16, PD, 128), b(16, PD, 128), b(16, PD, 128), b(16, PD, 128)]
        + [b(LEARN, PU, 128), b(LEARN, PU, 128), b(LEARN, PU, 128)]
        + [b(2, PW, 128), b(LEARN, PW, 128), b(RANK, WCOLS)]
        + [pltpu.SemaphoreType.DMA((9,)), pltpu.SemaphoreType.DMA((7,))]
        + [pltpu.SemaphoreType.DMA((16,)), pltpu.SemaphoreType.DMA((16,))],
        compiler_params=pltpu.CompilerParams(
            collective_id=0, has_side_effects=True, vmem_limit_bytes=60 * 2**20
        ),
        cost_estimate=pl.CostEstimate(
            flops=10**9, bytes_accessed=6 * 10**6, transcendentals=0
        ),
        name="adapter_step",
    )(*args))


def solution(mesh):
    return jax.shard_map(
        per_device,
        mesh=mesh,
        in_specs=(P("roll", "learn"),) + (P("learn", "roll"),) * 8,
        out_specs=(P("roll", "learn"),) + (P("learn", "roll"),) * 6,
        check_vma=False,
    )
```

```python
import math

import jax
import jax.numpy as jnp
from jax import lax
from jax.experimental import pallas as pl
from jax.experimental.pallas import tpu as pltpu
from jax.sharding import PartitionSpec as P

MESH = pl.DeviceIdType.MESH
BF16, F32 = jnp.bfloat16, jnp.float32

LEARN, ROLL, NZ, NX, NH = 32, 16, 8, 4, 4
RANK, TOKENS, OWN = 128, 20480, 4
ROWS, HID, OUT, WCOLS = 640, 1792, 512, 896
PART = ROWS // NX
TD, TU, TW = HID // 128, OUT // 128, WCOLS // 128
PD, PU, PW = 64, 16, 32

STEP = 20
adapter_scale = 2.0
learning_rate = 0.001
beta_one = 0.9
beta_two = 0.999
epsilon = 1e-08
weight_decay = 0.01


def adam(weights, moment_one, moment_two, gradient):
    one_next = beta_one * moment_one + (1.0 - beta_one) * gradient
    two_next = beta_two * moment_two + (1.0 - beta_two) * gradient * gradient
    corr_one = 1.0 - beta_one**STEP
    corr_two = 1.0 - beta_two**STEP
    update = one_next / corr_one / (jnp.sqrt(two_next / corr_two) + epsilon)
    return weights - learning_rate * (update + weight_decay * weights), one_next, two_next


def onehot(rows, cols, column_of_row):
    row = lax.broadcasted_iota(jnp.int32, (rows, cols), 0)
    col = lax.broadcasted_iota(jnp.int32, (rows, cols), 1)
    return jnp.where(column_of_row(row) == col, 1.0, 0.0).astype(BF16)


def dot(a, b, ca, cb):
    return lax.dot_general(a, b, (((ca,), (cb,)), ((), ())), preferred_element_type=F32)


def pack(value, tiles, rows):
    parts = [value[:, 128 * t : 128 * t + 128] for t in range(tiles)]
    if rows > OWN * tiles:
        parts.append(jnp.zeros((rows - OWN * tiles, 128), value.dtype))
    return jnp.concatenate(parts, axis=0).astype(BF16)


def unpack(value, tiles):
    return jnp.concatenate([value[OWN * t : OWN * t + OWN] for t in range(tiles)], axis=1)


def kernel(
    w_hbm, x_hbm, g_hbm, dp_hbm, dm_hbm, dv_hbm, up_hbm, um_hbm, uv_hbm,
    w_v, umat, dnew, dpo, dmo, dvo, upo, umo, uvo,
    x_v, g_v, dp_v, dm_v, dv_v, up_v, um_v, uv_v,
    ubuf, dbuf, dmat, pu, pd, pdt, put, pw,
    bpart, bx, bh, blow, hpart, hx, hh, hlow,
    gpack, gcore, gsum, gz, upack, ured, unew, fsend, fbuf,
    load_sem, send_sem, recv_sem,
):
    l = lax.axis_index("learn")
    r = lax.axis_index("roll")
    z, zy, q, core = l // 4, l // 2, l % 4, l % 2
    yhi, x = r // 4, r % 4
    core_peer = (l + 1 - 2 * core, r)
    ylo_peer = (l + 2 - 4 * (q // 2), r)
    source_roll = l // 2
    at_home = r == source_roll

    barrier = pltpu.get_barrier_semaphore()

    def greet(to):
        pl.semaphore_signal(barrier, inc=1, device_id=to, device_id_type=MESH)

    for k in range(1, LEARN):
        greet(((l + k) % LEARN, r))
    for k in range(1, 4):
        greet((l, yhi * 4 + (x + k) % 4))
        greet((l, ((yhi + k) % 4) * 4 + x))
    for k in range(LEARN):
        greet(((l + k) % LEARN, source_roll))

    loads = []
    for k, (src, dst) in enumerate(
        [(up_hbm, up_v), (dp_hbm, dp_v), (g_hbm, g_v), (x_hbm, x_v), (dm_hbm, dm_v), (dv_hbm, dv_v),
         (um_hbm, um_v), (uv_hbm, uv_v), (w_hbm, w_v)]
    ):
        copy = pltpu.make_async_copy(src, dst, load_sem.at[k])
        copy.start()
        loads.append(copy)
    load_up, load_dp, load_g, load_x = loads[:4]

    load_up.wait()
    load_dp.wait()
    ubuf[l] = pack(up_v[...], TU, PU)
    dbuf[q, z] = pack(dp_v[...], TD, PD)
    pl.semaphore_wait(barrier, LEARN - 1 + 6 + LEARN)

    arriving, leaving = {}, []

    def rcopy(src, dst, k, to):
        return pltpu.make_async_remote_copy(
            src_ref=src, dst_ref=dst, send_sem=send_sem.at[k], recv_sem=recv_sem.at[k],
            device_id=to, device_id_type=MESH,
        )

    def drain(ref, sem):
        pltpu.make_async_copy(ref, ref, sem).wait()

    def sent(k, ref):
        arriving[k] = ref
        leaving.append((k, ref))

    def receive(k):
        drain(arriving.pop(k), recv_sem.at[k])

    def finish():
        for k in list(arriving):
            receive(k)
        for k, ref in leaving:
            if k != 14:
                drain(ref, send_sem.at[k])
        if any(k == 14 for k, _ in leaving):
            drain(fbuf.at[pl.ds(0, LEARN - 1)], send_sem.at[14])

            @pl.when(jnp.logical_not(at_home))
            def _():
                drain(fbuf.at[0], send_sem.at[14])

    def learn_all(src_of, dst, k):
        def send(j, c):
            to = (l + j) % LEARN
            rcopy(src_of(to), dst.at[l], k, (to, r)).start()
            return c

        lax.fori_loop(1, LEARN, send, 0)
        sent(k, dst.at[pl.ds(0, LEARN - 1)])

    def x_to(j):
        return yhi * 4 + (x + j) % 4

    def h_to(j):
        return ((yhi + j) % 4) * 4 + x

    learn_all(lambda to: ubuf.at[l], ubuf, 0)
    for j in range(1, NZ):
        rcopy(dbuf.at[q, z], dbuf.at[q, z], 1, (((z + j) % NZ) * 4 + q, r)).start()
    sent(1, dbuf.at[0, pl.ds(0, NZ - 1)])

    pu[...] = onehot(512, 512, lambda a: ((a & 127) >> 2) * 16 + (a >> 7) * 4 + (a & 3))
    pd[...] = onehot(448, 512, lambda a: ((a & 31) >> 2) * 64 + (a >> 5) * 4 + (a & 3))
    pdt[...] = onehot(
        512, 448,
        lambda a: jnp.where(
            (a & 63) < 56,
            ((a & 63) >> 2) * 32 + ((a >> 6) & 3) * 8 + (a >> 8) * 4 + (a & 3),
            -1,
        ),
    )
    put[...] = onehot(
        512, 512,
        lambda a: ((a & 15) >> 2) * 128 + ((a >> 4) & 3) * 32 + (a >> 6) * 4 + (a & 3),
    )

    pw[...] = onehot(448, 512, lambda a: ((a & 63) >> 2) * 32 + (a >> 6) * 4 + (a & 3))

    receive(0)
    spread = dot(pu[...], ubuf[...].reshape(512, 128), 1, 0).astype(BF16)
    for t in range(TU):
        umat[:, 128 * t : 128 * t + 128] = spread[128 * t : 128 * t + 128]
    load_g.wait()
    bpart[...] = dot(g_v[...], umat[...], 1, 1).astype(BF16).reshape(NX, PART, 128)
    for j in range(1, 4):
        rcopy(bpart.at[(x + j) % 4], bx.at[x], 2, (l, x_to(j))).start()
    sent(2, bx.at[pl.ds(0, 3)])
    bx[x] = bpart[x]

    receive(1)
    rcopy(dbuf.at[q], dbuf.at[q], 3, core_peer).start()
    sent(3, dbuf.at[0])
    rcopy(dbuf.at[q], dbuf.at[q], 4, ylo_peer).start()
    sent(4, dbuf.at[0])

    def sum_four(buf):
        v = buf[...].astype(F32)
        return (v[0] + v[1]) + (v[2] + v[3])

    receive(2)
    bh[yhi] = sum_four(bx).astype(BF16)
    for j in range(1, 4):
        rcopy(bh.at[yhi], bh.at[yhi], 5, (l, h_to(j))).start()
    sent(5, bh.at[pl.ds(0, 3)])

    receive(4)
    q_other = (q + 2) % 4
    rcopy(dbuf.at[q_other], dbuf.at[q_other], 6, core_peer).start()
    sent(6, dbuf.at[0])
    receive(3)
    receive(6)
    for k in range(4):
        spread = dot(pd[...], dbuf[k].reshape(512, 128), 1, 0).astype(BF16)
        for t in range(TD):
            dmat[32 * k : 32 * k + 32, 128 * t : 128 * t + 128] = spread[32 * t : 32 * t + 32]
    load_x.wait()
    hpart[...] = dot(x_v[...], dmat[...], 1, 1).astype(BF16).reshape(NX, PART, 128)
    for j in range(1, 4):
        rcopy(hpart.at[(x + j) % 4], hx.at[x], 7, (l, x_to(j))).start()
    sent(7, hx.at[pl.ds(0, 3)])
    hx[x] = hpart[x]

    receive(5)
    blow[x] = (adapter_scale * sum_four(bh)).astype(BF16)
    for j in range(1, 4):
        rcopy(blow.at[x], blow.at[x], 8, (l, x_to(j))).start()
    sent(8, blow.at[pl.ds(0, 3)])

    receive(7)
    hh[yhi] = sum_four(hx).astype(BF16)
    for j in range(1, 4):
        rcopy(hh.at[yhi], hh.at[yhi], 9, (l, h_to(j))).start()
    sent(9, hh.at[pl.ds(0, 3)])

    normalizer_scale = 1.0 / math.sqrt(TOKENS)
    receive(8)
    grad = (normalizer_scale * dot(blow[...].reshape(ROWS, 128), x_v[...], 0, 0)).astype(BF16)
    for k in range(4):
        stack = jnp.concatenate(
            [grad[32 * k : 32 * k + 32, 128 * t : 128 * t + 128] for t in range(TD)], axis=0
        )
        packed = dot(pdt[...], stack, 1, 0).astype(BF16)
        gpack[0, 4 * k : 4 * k + 4] = packed[:256].reshape(4, PD, 128)
        gpack[1, 4 * k : 4 * k + 4] = packed[256:].reshape(4, PD, 128)
    rcopy(gpack.at[1 - core], gcore, 10, core_peer).start()
    sent(10, gcore)

    receive(9)
    hlow[x] = sum_four(hh).astype(BF16)
    for j in range(1, 4):
        rcopy(hlow.at[x], hlow.at[x], 11, (l, x_to(j))).start()
    sent(11, hlow.at[pl.ds(0, 3)])

    receive(10)
    gsum[...] = (gpack[core].astype(F32) + gcore[...].astype(F32)).astype(BF16)

    def send_gsum(j, c):
        to = (zy + j) % 16
        rcopy(gsum.at[to], gz.at[zy], 12, (to * 2 + core, r)).start()
        return c

    lax.fori_loop(1, 16, send_gsum, 0)
    sent(12, gz.at[pl.ds(0, 15)])
    gz[zy] = gsum[zy]

    receive(11)
    gradu = (adapter_scale * normalizer_scale) * dot(hlow[...].reshape(ROWS, 128), g_v[...], 0, 0)
    gradu = gradu.astype(BF16)
    stack = jnp.concatenate([gradu[:, 128 * t : 128 * t + 128] for t in range(TU)], axis=0)
    upack[...] = dot(put[...], stack, 1, 0).astype(BF16).reshape(LEARN, PU, 128)
    learn_all(lambda to: upack.at[to], ured, 13)
    ured[l] = upack[l]

    for copy in loads[4:]:
        copy.wait()
    receive(12)
    gradient = unpack(jnp.sum(gz[...].astype(F32), axis=0), TD)
    new_p, new_m, new_v = adam(dp_v[...], dm_v[...], dv_v[...], gradient)
    fsend[0] = pack(new_p[:, :WCOLS], TW, PW)
    fsend[1] = pack(new_p[:, WCOLS:], TW, PW)

    def send_shard(k, c):
        to_l, to_r = 2 * r + k // 16, k % 16
        own = jnp.logical_and(to_l == l, to_r == r)

        @pl.when(jnp.logical_not(own))
        def _():
            rcopy(fsend.at[k // 16], fbuf.at[l], 14, (to_l, to_r)).start()

        @pl.when(own)
        def _():
            pltpu.make_async_copy(fsend.at[k // 16], fbuf.at[l], recv_sem.at[14]).start()

        return c

    lax.fori_loop(0, 32, send_shard, 0)
    sent(14, fbuf)
    dpo[...] = new_p
    dmo[...] = new_m
    dvo[...] = new_v

    receive(13)
    gradient = unpack(jnp.sum(ured[...].astype(F32), axis=0), TU)
    new_p, new_m, new_v = adam(up_v[...], um_v[...], uv_v[...], gradient)
    unew[l] = pack(new_p, TU, PU)
    learn_all(lambda to: unew.at[l], unew, 15)

    upo[...] = new_p
    umo[...] = new_m
    uvo[...] = new_v

    receive(14)
    for k in range(2):
        spread = dot(pw[...], fbuf[16 * k : 16 * k + 16].reshape(512, 128), 1, 0).astype(BF16)
        for t in range(TW):
            dnew[64 * k : 64 * k + 64, 128 * t : 128 * t + 128] = spread[64 * t : 64 * t + 64]
    receive(15)
    spread = dot(pu[...], unew[...].reshape(512, 128), 1, 0).astype(BF16)
    for t in range(TU):
        umat[:, 128 * t : 128 * t + 128] = spread[128 * t : 128 * t + 128]
    finish()


def merge_kernel(w, umat, dnew, *refs):
    moved, wo_hbm, stored, wo_v, store_sem = refs[:6], refs[6], refs[7:13], refs[13], refs[14]
    stores = []

    def store(src, dst):
        copy = pltpu.make_async_copy(src, dst, store_sem.at[len(stores)])
        copy.start()
        stores.append(copy)

    for src, dst in zip(moved, stored):
        store(src, dst)
    for k in range(4):
        rows = slice(128 * k, 128 * k + 128)
        product = dot(umat[:, rows], dnew[...], 0, 0)
        wo_v[rows] = (w[rows].astype(F32) + adapter_scale * product).astype(BF16)
        store(wo_v.at[rows], wo_hbm.at[rows])
    for copy in stores:
        copy.wait()


def per_device(*args):
    down, up = (OWN, HID), (OWN, OUT)
    small = [down, down, down, up, up, up]
    hbm = pl.BlockSpec(memory_space=pltpu.HBM)
    vmem = pl.BlockSpec(memory_space=pltpu.VMEM)
    dma = pltpu.SemaphoreType.DMA

    def b(*shape):
        return pltpu.VMEM(shape, BF16)

    states = [jax.ShapeDtypeStruct(s, F32) for s in small]
    low = [b(NX, PART, 128) for _ in range(4)]
    made = pl.pallas_call(
        kernel,
        out_shape=[
            jax.ShapeDtypeStruct((OUT, WCOLS), BF16),
            jax.ShapeDtypeStruct((RANK, OUT), BF16),
            jax.ShapeDtypeStruct((RANK, WCOLS), BF16),
        ]
        + states,
        in_specs=[hbm] * 9,
        out_specs=[vmem] * 9,
        scratch_shapes=[b(ROWS, HID), b(ROWS, OUT)]
        + [pltpu.VMEM(s, F32) for s in small]
        + [b(LEARN, PU, 128), b(4, NZ, PD, 128), b(RANK, HID)]
        + [b(512, 512), b(448, 512), b(512, 448), b(512, 512), b(448, 512)]
        + low
        + low
        + [b(2, 16, PD, 128), b(16, PD, 128), b(16, PD, 128), b(16, PD, 128)]
        + [b(LEARN, PU, 128), b(LEARN, PU, 128), b(LEARN, PU, 128)]
        + [b(2, PW, 128), b(LEARN, PW, 128)]
        + [dma((9,)), dma((16,)), dma((16,))],
        compiler_params=pltpu.CompilerParams(
            collective_id=0, has_side_effects=True, vmem_limit_bytes=40 * 2**20
        ),
        cost_estimate=pl.CostEstimate(flops=10**9, bytes_accessed=10**7, transcendentals=0),
        name="adapter_step",
    )(*(pltpu.with_memory_space_constraint(a, pltpu.HBM) for a in args))
    return tuple(
        pl.pallas_call(
            merge_kernel,
            out_shape=[jax.ShapeDtypeStruct((OUT, WCOLS), BF16)] + states,
            in_specs=[vmem] * 9,
            out_specs=[hbm] * 7,
            scratch_shapes=[b(OUT, WCOLS), dma((10,))],
            compiler_params=pltpu.CompilerParams(vmem_limit_bytes=20 * 2**20),
            cost_estimate=pl.CostEstimate(flops=10**8, bytes_accessed=2 * 10**6, transcendentals=0),
            name="merge",
        )(*made)
    )


def solution(mesh):
    return jax.shard_map(
        per_device,
        mesh=mesh,
        in_specs=(P("roll", "learn"),) + (P("learn", "roll"),) * 8,
        out_specs=(P("roll", "learn"),) + (P("learn", "roll"),) * 6,
        check_vma=False,
    )
```

```python
import math

import jax
import jax.numpy as jnp
from jax import lax
from jax.experimental import pallas as pl
from jax.experimental.pallas import tpu as pltpu
from jax.sharding import PartitionSpec as P

MESH = pl.DeviceIdType.MESH
BF16, F32 = jnp.bfloat16, jnp.float32

LEARN, ROLL, NX = 32, 16, 4
FAR_FIRST = (10, 6, 14, 9, 11, 8, 5, 7, 13, 15, 4, 12, 2, 1, 3)
RANK, TOKENS, OWN = 128, 20480, 4
ROWS, HID, OUT, WCOLS = 640, 1792, 512, 896
PART = ROWS // NX
TD, TU, TW = HID // 128, OUT // 128, WCOLS // 128
PD, PU, PW = 64, 16, 32

STEP = 20
adapter_scale = 2.0
learning_rate = 0.001
beta_one = 0.9
beta_two = 0.999
epsilon = 1e-08
weight_decay = 0.01


def adam(weights, moment_one, moment_two, gradient):
    one_next = beta_one * moment_one + (1.0 - beta_one) * gradient
    two_next = beta_two * moment_two + (1.0 - beta_two) * gradient * gradient
    corr_one = 1.0 - beta_one**STEP
    corr_two = 1.0 - beta_two**STEP
    update = one_next / corr_one / (jnp.sqrt(two_next / corr_two) + epsilon)
    return weights - learning_rate * (update + weight_decay * weights), one_next, two_next


def onehot(rows, cols, column_of_row):
    row = lax.broadcasted_iota(jnp.int32, (rows, cols), 0)
    col = lax.broadcasted_iota(jnp.int32, (rows, cols), 1)
    return jnp.where(column_of_row(row) == col, 1.0, 0.0).astype(BF16)


def dot(a, b, ca, cb):
    return lax.dot_general(a, b, (((ca,), (cb,)), ((), ())), preferred_element_type=F32)


def pack(value, tiles, rows):
    parts = [value[:, 128 * t : 128 * t + 128] for t in range(tiles)]
    if rows > OWN * tiles:
        parts.append(jnp.zeros((rows - OWN * tiles, 128), value.dtype))
    return jnp.concatenate(parts, axis=0).astype(BF16)


def unpack(value, tiles):
    return jnp.concatenate([value[OWN * t : OWN * t + OWN] for t in range(tiles)], axis=1)


def kernel(
    w_hbm, x_hbm, g_hbm, dp_hbm, dm_hbm, dv_hbm, up_hbm, um_hbm, uv_hbm,
    w_v, umat, dnew, dpo, dmo, dvo, upo, umo, uvo,
    x_v, g_v, dp_v, dm_v, dv_v, up_v, um_v, uv_v,
    ubuf, dbuf, dmat, pu, pd, pdt, put, pw,
    bpart, bx, bh, blow, hpart, hx, hh, hlow,
    gpack, gcore, gsum, gz, upack, ured, unew, fgat, fbuf,
    load_sem, send_sem, recv_sem, roll_sem,
):
    l = lax.axis_index("learn")
    r = lax.axis_index("roll")
    zy, core = l // 2, l % 2
    yhi, x = r // 4, r % 4
    core_peer = (l + 1 - 2 * core, r)
    slot = core * 16 + zy

    barrier = pltpu.get_barrier_semaphore()

    def greet(to):
        pl.semaphore_signal(barrier, inc=1, device_id=to, device_id_type=MESH)

    for k in range(1, LEARN):
        greet(((l + k) % LEARN, r))
    for k in range(1, ROLL):
        greet((l, (r + k) % ROLL))

    loads = []
    for k, (src, dst) in enumerate(
        [(up_hbm, up_v), (dp_hbm, dp_v), (g_hbm, g_v), (x_hbm, x_v), (dm_hbm, dm_v), (dv_hbm, dv_v),
         (um_hbm, um_v), (uv_hbm, uv_v), (w_hbm, w_v)]
    ):
        copy = pltpu.make_async_copy(src, dst, load_sem.at[k])
        copy.start()
        loads.append(copy)
    load_up, load_dp, load_g, load_x = loads[:4]

    load_up.wait()
    load_dp.wait()
    ubuf[slot] = pack(up_v[...], TU, PU)
    dbuf[slot] = pack(dp_v[...], TD, PD)
    pl.semaphore_wait(barrier, LEARN + ROLL - 2)

    arriving, leaving = {}, []

    def rcopy(src, dst, k, to, sem=None):
        return pltpu.make_async_remote_copy(
            src_ref=src, dst_ref=dst, send_sem=send_sem.at[k],
            recv_sem=recv_sem.at[k] if sem is None else sem,
            device_id=to, device_id_type=MESH,
        )

    def drain(ref, sem):
        pltpu.make_async_copy(ref, ref, sem).wait()

    def sent(k, ref):
        arriving[k] = ref
        leaving.append((k, ref))

    def receive(k):
        drain(arriving.pop(k), recv_sem.at[k])

    def finish():
        for k in list(arriving):
            receive(k)
        for k, ref in leaving:
            drain(ref, send_sem.at[k])

    def learn_all(src_of, dst, k):
        def send(j, c):
            to = (l + j) % LEARN
            rcopy(src_of(to), dst, k, (to, r)).start()
            return c

        lax.fori_loop(1, LEARN, send, 0)

    def zy_all(src_of, dst, k):
        def send(j, c):
            to = (zy + j) % 16
            rcopy(src_of(to), dst, k, (to * 2 + core, r)).start()
            return c

        lax.fori_loop(1, 16, send, 0)

    def x_to(j):
        return yhi * 4 + (x + j) % 4

    def h_to(j):
        return ((yhi + j) % 4) * 4 + x

    def x_all(src_of, dst, buf, k):
        for j in (2, 1, 3):
            rcopy(src_of((x + j) % 4), dst, k, (l, x_to(j))).start()
        sent(k, buf.at[pl.ds(0, 3)])

    def h_all(src, dst, buf, k):
        for j in (2, 1, 3):
            rcopy(src, dst, k, (l, h_to(j))).start()
        sent(k, buf.at[pl.ds(0, 3)])

    zy_all(lambda to: ubuf.at[slot], ubuf.at[slot], 0)
    sent(0, ubuf.at[pl.ds(0, 15)])
    zy_all(lambda to: dbuf.at[slot], dbuf.at[slot], 1)
    sent(1, dbuf.at[pl.ds(0, 15)])
    half = pl.ds(core * 16, 16)

    pu[...] = onehot(
        512, 512, lambda a: ((a >> 2) & 1) * 256 + ((a & 127) >> 3) * 16 + (a >> 7) * 4 + (a & 3)
    )
    pd[...] = onehot(448, 512, lambda a: ((a & 31) >> 2) * 64 + (a >> 5) * 4 + (a & 3))
    pdt[...] = onehot(
        512, 448,
        lambda a: jnp.where(
            (a & 63) < 56,
            ((a & 63) >> 2) * 32 + ((a >> 6) & 3) * 8 + (a >> 8) * 4 + (a & 3),
            -1,
        ),
    )
    put[...] = onehot(
        512, 512,
        lambda a: ((a & 15) >> 2) * 128 + ((a >> 4) & 1) * 64 + (a >> 5) * 4 + (a & 3),
    )
    pw[...] = onehot(448, 512, lambda a: ((a & 63) >> 2) * 32 + (a >> 6) * 4 + (a & 3))

    def unpack_up(buf):
        spread = dot(pu[...], buf[...].reshape(512, 128), 1, 0).astype(BF16)
        for t in range(TU):
            umat[:, 128 * t : 128 * t + 128] = spread[128 * t : 128 * t + 128]

    def sum_four(buf):
        v = buf[...].astype(F32)
        return (v[0] + v[1]) + (v[2] + v[3])

    receive(0)
    rcopy(ubuf.at[half], ubuf.at[half], 2, core_peer).start()
    sent(2, ubuf.at[pl.ds(0, 16)])
    load_g.wait()
    receive(2)
    unpack_up(ubuf)
    bpart[...] = dot(g_v[...], umat[...], 1, 1).astype(BF16).reshape(NX, PART, 128)
    x_all(lambda to: bpart.at[to], bx.at[x], bx, 3)
    bx[x] = bpart[x]

    receive(1)
    rcopy(dbuf.at[half], dbuf.at[half], 4, core_peer).start()
    sent(4, dbuf.at[pl.ds(0, 16)])
    load_x.wait()
    receive(4)
    for k in range(4):
        spread = dot(pd[...], dbuf[8 * k : 8 * k + 8].reshape(512, 128), 1, 0).astype(BF16)
        for t in range(TD):
            dmat[32 * k : 32 * k + 32, 128 * t : 128 * t + 128] = spread[32 * t : 32 * t + 32]
    hpart[...] = dot(x_v[...], dmat[...], 1, 1).astype(BF16).reshape(NX, PART, 128)
    x_all(lambda to: hpart.at[to], hx.at[x], hx, 5)
    hx[x] = hpart[x]

    receive(3)
    bh[yhi] = sum_four(bx).astype(BF16)
    h_all(bh.at[yhi], bh.at[yhi], bh, 6)
    receive(5)
    hh[yhi] = sum_four(hx).astype(BF16)
    h_all(hh.at[yhi], hh.at[yhi], hh, 7)
    receive(6)
    blow[x] = (adapter_scale * sum_four(bh)).astype(BF16)
    x_all(lambda to: blow.at[x], blow.at[x], blow, 8)

    normalizer_scale = 1.0 / math.sqrt(TOKENS)
    receive(8)
    grad = (normalizer_scale * dot(blow[...].reshape(ROWS, 128), x_v[...], 0, 0)).astype(BF16)
    for k in range(4):
        stack = jnp.concatenate(
            [grad[32 * k : 32 * k + 32, 128 * t : 128 * t + 128] for t in range(TD)], axis=0
        )
        packed = dot(pdt[...], stack, 1, 0).astype(BF16)
        gpack[0, 4 * k : 4 * k + 4] = packed[:256].reshape(4, PD, 128)
        gpack[1, 4 * k : 4 * k + 4] = packed[256:].reshape(4, PD, 128)
    rcopy(gpack.at[1 - core], gcore, 10, core_peer).start()
    sent(10, gcore)

    receive(7)
    hlow[x] = sum_four(hh).astype(BF16)
    x_all(lambda to: hlow.at[x], hlow.at[x], hlow, 9)

    receive(10)
    gsum[...] = (gpack[core].astype(F32) + gcore[...].astype(F32)).astype(BF16)
    zy_all(lambda to: gsum.at[to], gz.at[zy], 12)
    sent(12, gz.at[pl.ds(0, 15)])
    gz[zy] = gsum[zy]

    receive(9)
    gradu = (adapter_scale * normalizer_scale) * dot(hlow[...].reshape(ROWS, 128), g_v[...], 0, 0)
    gradu = gradu.astype(BF16)
    stack = jnp.concatenate([gradu[:, 128 * t : 128 * t + 128] for t in range(TU)], axis=0)
    upack[...] = dot(put[...], stack, 1, 0).astype(BF16).reshape(LEARN, PU, 128)
    learn_all(lambda to: upack.at[to], ured.at[l], 13)
    sent(13, ured.at[pl.ds(0, LEARN - 1)])
    ured[l] = upack[l]

    for copy in loads[4:]:
        copy.wait()
    receive(12)
    gradient = unpack(jnp.sum(gz[...].astype(F32), axis=0), TD)
    new_p, new_m, new_v = adam(dp_v[...], dm_v[...], dv_v[...], gradient)
    fgat[r, pl.ds(0, PW)] = pack(new_p[:, :WCOLS], TW, PW)
    fgat[r, pl.ds(PW, PW)] = pack(new_p[:, WCOLS:], TW, PW)
    for j in FAR_FIRST:
        to = (yhi + j // 4) % 4 * 4 + (x + j % 4) % 4
        rcopy(fgat.at[r], fgat.at[r], 14, (l, to), roll_sem.at[r]).start()
    leaving.append((14, fgat.at[pl.ds(0, ROLL - 1)]))
    dpo[...] = new_p
    dmo[...] = new_m
    dvo[...] = new_v

    receive(13)
    gradient = unpack(jnp.sum(ured[...].astype(F32), axis=0), TU)
    new_p, new_m, new_v = adam(up_v[...], um_v[...], uv_v[...], gradient)
    unew[slot] = pack(new_p, TU, PU)
    learn_all(lambda to: unew.at[slot], unew.at[slot], 15)
    sent(15, unew.at[pl.ds(0, LEARN - 1)])
    upo[...] = new_p
    umo[...] = new_m
    uvo[...] = new_v

    for j in (0,) + FAR_FIRST[::-1]:
        piece = (yhi + j // 4) % 4 * 4 + (x + j % 4) % 4
        if j:
            drain(fgat.at[piece], roll_sem.at[piece])
        near, far = fgat.at[piece, pl.ds(core * PW, PW)], fgat.at[piece, pl.ds((1 - core) * PW, PW)]
        rcopy(far, fbuf.at[l], 16, (2 * piece + 1 - core, r)).start()

        @pl.when(piece != zy)
        def _():
            rcopy(near, fbuf.at[l], 16, (2 * piece + core, r)).start()

        @pl.when(piece == zy)
        def _():
            pltpu.make_async_copy(near, fbuf.at[l], recv_sem.at[16]).start()

    arriving[16] = fbuf
    leaving.append((16, fbuf.at[pl.ds(0, LEARN - 1)]))

    receive(16)
    for k in range(2):
        spread = dot(pw[...], fbuf[16 * k : 16 * k + 16].reshape(512, 128), 1, 0).astype(BF16)
        for t in range(TW):
            dnew[64 * k : 64 * k + 64, 128 * t : 128 * t + 128] = spread[64 * t : 64 * t + 64]
    receive(15)
    unpack_up(unew)
    finish()


def merge_kernel(w, umat, dnew, *refs):
    moved, wo_hbm, stored, wo_v, store_sem = refs[:6], refs[6], refs[7:13], refs[13], refs[14]
    stores = []

    def store(src, dst):
        copy = pltpu.make_async_copy(src, dst, store_sem.at[len(stores)])
        copy.start()
        stores.append(copy)

    for src, dst in zip(moved, stored):
        store(src, dst)
    for k in range(4):
        rows = slice(128 * k, 128 * k + 128)
        product = dot(umat[:, rows], dnew[...], 0, 0)
        wo_v[rows] = (w[rows].astype(F32) + adapter_scale * product).astype(BF16)
        store(wo_v.at[rows], wo_hbm.at[rows])
    for copy in stores:
        copy.wait()


def per_device(*args):
    down, up = (OWN, HID), (OWN, OUT)
    small = [down, down, down, up, up, up]
    hbm = pl.BlockSpec(memory_space=pltpu.HBM)
    vmem = pl.BlockSpec(memory_space=pltpu.VMEM)
    dma = pltpu.SemaphoreType.DMA

    def b(*shape):
        return pltpu.VMEM(shape, BF16)

    states = [jax.ShapeDtypeStruct(s, F32) for s in small]
    low = [b(NX, PART, 128) for _ in range(4)]
    made = pl.pallas_call(
        kernel,
        out_shape=[
            jax.ShapeDtypeStruct((OUT, WCOLS), BF16),
            jax.ShapeDtypeStruct((RANK, OUT), BF16),
            jax.ShapeDtypeStruct((RANK, WCOLS), BF16),
        ]
        + states,
        in_specs=[hbm] * 9,
        out_specs=[vmem] * 9,
        scratch_shapes=[b(ROWS, HID), b(ROWS, OUT)]
        + [pltpu.VMEM(s, F32) for s in small]
        + [b(LEARN, PU, 128), b(LEARN, PD, 128), b(RANK, HID)]
        + [b(512, 512), b(448, 512), b(512, 448), b(512, 512), b(448, 512)]
        + low
        + low
        + [b(2, 16, PD, 128), b(16, PD, 128), b(16, PD, 128), b(16, PD, 128)]
        + [b(LEARN, PU, 128), b(LEARN, PU, 128), b(LEARN, PU, 128)]
        + [b(ROLL, 2 * PW, 128), b(LEARN, PW, 128)]
        + [dma((9,)), dma((17,)), dma((17,)), dma((ROLL,))],
        compiler_params=pltpu.CompilerParams(
            collective_id=0, has_side_effects=True, vmem_limit_bytes=40 * 2**20
        ),
        cost_estimate=pl.CostEstimate(flops=10**9, bytes_accessed=10**7, transcendentals=0),
        name="adapter_step",
    )(*(pltpu.with_memory_space_constraint(a, pltpu.HBM) for a in args))
    return tuple(
        pl.pallas_call(
            merge_kernel,
            out_shape=[jax.ShapeDtypeStruct((OUT, WCOLS), BF16)] + states,
            in_specs=[vmem] * 9,
            out_specs=[hbm] * 7,
            scratch_shapes=[b(OUT, WCOLS), dma((10,))],
            compiler_params=pltpu.CompilerParams(vmem_limit_bytes=20 * 2**20),
            cost_estimate=pl.CostEstimate(flops=10**8, bytes_accessed=2 * 10**6, transcendentals=0),
            name="merge",
        )(*made)
    )


def solution(mesh):
    return jax.shard_map(
        per_device,
        mesh=mesh,
        in_specs=(P("roll", "learn"),) + (P("learn", "roll"),) * 8,
        out_specs=(P("roll", "learn"),) + (P("learn", "roll"),) * 6,
        check_vma=False,
    )
```

```python
import math

import jax
import jax.numpy as jnp
from jax import lax
from jax.experimental import pallas as pl
from jax.experimental.pallas import tpu as pltpu
from jax.sharding import PartitionSpec as P

MESH = pl.DeviceIdType.MESH
BF16, F32 = jnp.bfloat16, jnp.float32

LEARN, ROLL, NX = 32, 16, 4
ZY_FAR_FIRST = tuple((dz, dp) for dz in (4, 3, 5, 2, 6, 1, 7) for dp in (1, 0)) + ((0, 1),)
FAR_FIRST = (10, 6, 14, 9, 11, 8, 5, 7, 13, 15, 4, 12, 2, 1, 3)
RANK, TOKENS, OWN = 128, 20480, 4
ROWS, HID, OUT, WCOLS = 640, 1792, 512, 896
PART = ROWS // NX
TD, TU, TW = HID // 128, OUT // 128, WCOLS // 128
PD, PU, PW = 64, 16, 32

STEP = 20
adapter_scale = 2.0
learning_rate = 0.001
beta_one = 0.9
beta_two = 0.999
epsilon = 1e-08
weight_decay = 0.01


def adam(weights, moment_one, moment_two, gradient):
    one_next = beta_one * moment_one + (1.0 - beta_one) * gradient
    two_next = beta_two * moment_two + (1.0 - beta_two) * gradient * gradient
    corr_one = 1.0 - beta_one**STEP
    corr_two = 1.0 - beta_two**STEP
    update = one_next / corr_one / (jnp.sqrt(two_next / corr_two) + epsilon)
    return weights - learning_rate * (update + weight_decay * weights), one_next, two_next


def dot(a, b, ca, cb):
    return lax.dot_general(a, b, (((ca,), (cb,)), ((), ())), preferred_element_type=F32)


def pack(value, tiles, rows):
    parts = [value[:, 128 * t : 128 * t + 128] for t in range(tiles)]
    if rows > OWN * tiles:
        parts.append(jnp.zeros((rows - OWN * tiles, 128), value.dtype))
    return jnp.concatenate(parts, axis=0).astype(BF16)


def rank_rows(of_core, tiles):
    halves = [of_core[c].astype(F32) for c in range(2)]
    return [
        jnp.concatenate([h[:, OWN * t : OWN * t + OWN] for h in halves], axis=1)
        .reshape(RANK, 128)
        .astype(BF16)
        for t in range(tiles)
    ]


def packed_rows(grad, core, pad):
    tiles = [
        grad[:, 128 * t : 128 * t + 128].reshape(16, 2 * OWN, 128)[:, OWN * core : OWN * core + OWN]
        for t in range(grad.shape[1] // 128)
    ]
    if pad:
        tiles.append(jnp.zeros((16, pad, 128), F32))
    return jnp.concatenate(tiles, axis=1).astype(BF16)


def unpack(value, tiles):
    return jnp.concatenate([value[OWN * t : OWN * t + OWN] for t in range(tiles)], axis=1)


def kernel(
    w_hbm, x_hbm, g_hbm, dp_hbm, dm_hbm, dv_hbm, up_hbm, um_hbm, uv_hbm,
    w_v, umat, dnew, dpo, dmo, dvo, upo, umo, uvo,
    x_v, g_v, dp_v, dm_v, dv_v, up_v, um_v, uv_v,
    ubuf, dbuf, dmat,
    bpart, bx, bh, blow, hpart, hx, hh, hlow,
    gpack, gcore, gsum, gz, upack, ucore, usum, uz, unew, fgat, fbuf,
    load_sem, send_sem, recv_sem, roll_sem,
):
    l = lax.axis_index("learn")
    r = lax.axis_index("roll")
    zy, core = l // 2, l % 2
    yhi, x = r // 4, r % 4
    core_peer = (l + 1 - 2 * core, r)
    slot = core * 16 + zy

    loads = []
    for k, (src, dst) in enumerate(
        [(up_hbm, up_v), (dp_hbm, dp_v), (g_hbm, g_v), (x_hbm, x_v), (dm_hbm, dm_v), (dv_hbm, dv_v),
         (um_hbm, um_v), (uv_hbm, uv_v), (w_hbm, w_v)]
    ):
        loads.append(pltpu.make_async_copy(src, dst, load_sem.at[k]))
    load_up, load_dp, load_g, load_x = loads[:4]
    load_up.start()
    load_dp.start()

    barrier = pltpu.get_barrier_semaphore()

    def greet(to):
        pl.semaphore_signal(barrier, inc=1, device_id=to, device_id_type=MESH)

    def zy_to(dz, dp):
        return ((zy // 2 + dz) % 8) * 2 + (zy + dp) % 2

    for dz, dp in ZY_FAR_FIRST:
        greet((zy_to(dz, dp) * 2 + core, r))
    for j in FAR_FIRST:
        greet((l, (yhi + j // 4) % 4 * 4 + (x + j % 4) % 4))
    for dz, dp in ZY_FAR_FIRST:
        greet((zy_to(dz, dp) * 2 + 1 - core, r))
    greet(core_peer)
    for copy in loads[2:]:
        copy.start()

    load_up.wait()
    load_dp.wait()
    ubuf[slot] = pack(up_v[...], TU, PU)
    dbuf[slot] = pack(dp_v[...], TD, PD)
    pl.semaphore_wait(barrier, LEARN + ROLL - 2)

    arriving, leaving = {}, []

    def rcopy(src, dst, k, to, sem=None):
        return pltpu.make_async_remote_copy(
            src_ref=src, dst_ref=dst, send_sem=send_sem.at[k],
            recv_sem=recv_sem.at[k] if sem is None else sem,
            device_id=to, device_id_type=MESH,
        )

    def drain(ref, sem):
        pltpu.make_async_copy(ref, ref, sem).wait()

    def sent(k, ref):
        arriving[k] = ref
        leaving.append((k, ref))

    def receive(k):
        drain(arriving.pop(k), recv_sem.at[k])

    def finish():
        for k in list(arriving):
            receive(k)
        for k, ref in leaving:
            drain(ref, send_sem.at[k])

    def zy_all(src_of, dst, k):
        for dz, dp in ZY_FAR_FIRST:
            to = zy_to(dz, dp)
            rcopy(src_of(to), dst, k, (to * 2 + core, r)).start()

    def x_to(j):
        return yhi * 4 + (x + j) % 4

    def h_to(j):
        return ((yhi + j) % 4) * 4 + x

    def x_all(src_of, dst, buf, k):
        for j in (2, 1, 3):
            rcopy(src_of((x + j) % 4), dst, k, (l, x_to(j))).start()
        sent(k, buf.at[pl.ds(0, 3)])

    def h_all(src, dst, buf, k):
        for j in (2, 1, 3):
            rcopy(src, dst, k, (l, h_to(j))).start()
        sent(k, buf.at[pl.ds(0, 3)])

    zy_all(lambda to: ubuf.at[slot], ubuf.at[slot], 0)
    sent(0, ubuf.at[pl.ds(0, 15)])
    zy_all(lambda to: dbuf.at[slot], dbuf.at[slot], 1)
    sent(1, dbuf.at[pl.ds(0, 15)])
    half = pl.ds(core * 16, 16)

    def unpack_up(buf):
        for t, rows in enumerate(rank_rows((buf[:16], buf[16:]), TU)):
            umat[:, 128 * t : 128 * t + 128] = rows

    def sum_four(buf):
        v = buf[...].astype(F32)
        return (v[0] + v[1]) + (v[2] + v[3])

    receive(0)
    rcopy(ubuf.at[half], ubuf.at[half], 2, core_peer).start()
    sent(2, ubuf.at[pl.ds(0, 16)])
    load_g.wait()
    receive(2)
    unpack_up(ubuf)
    bpart[...] = dot(g_v[...], umat[...], 1, 1).astype(BF16).reshape(NX, PART, 128)
    x_all(lambda to: bpart.at[to], bx.at[x], bx, 3)
    bx[x] = bpart[x]

    receive(1)
    rcopy(dbuf.at[half], dbuf.at[half], 4, core_peer).start()
    sent(4, dbuf.at[pl.ds(0, 16)])
    load_x.wait()
    receive(4)
    for k in range(0, TD, 4):
        packed = dbuf[:, OWN * k : OWN * k + 16]
        for t, rows in enumerate(rank_rows((packed[:16], packed[16:]), min(4, TD - k))):
            dmat[:, 128 * (k + t) : 128 * (k + t) + 128] = rows
    hpart[...] = dot(x_v[...], dmat[...], 1, 1).astype(BF16).reshape(NX, PART, 128)
    x_all(lambda to: hpart.at[to], hx.at[x], hx, 5)
    hx[x] = hpart[x]

    receive(3)
    bh[yhi] = sum_four(bx).astype(BF16)
    h_all(bh.at[yhi], bh.at[yhi], bh, 6)
    receive(5)
    hh[yhi] = sum_four(hx).astype(BF16)
    h_all(hh.at[yhi], hh.at[yhi], hh, 7)
    receive(6)
    blow[x] = (adapter_scale * sum_four(bh)).astype(BF16)
    x_all(lambda to: blow.at[x], blow.at[x], blow, 8)

    normalizer_scale = 1.0 / math.sqrt(TOKENS)
    receive(8)
    low = blow[...].reshape(ROWS, 128)
    for k in range(0, TD, 4):
        tiles = min(4, TD - k)
        grad = normalizer_scale * dot(low, x_v[:, 128 * k : 128 * (k + tiles)], 0, 0)
        for c in range(2):
            gpack[c, :, OWN * k : OWN * k + 16] = packed_rows(grad, c, 16 - OWN * tiles)
    rcopy(gpack.at[1 - core], gcore, 10, core_peer).start()
    sent(10, gcore)

    receive(7)
    hlow[x] = sum_four(hh).astype(BF16)
    x_all(lambda to: hlow.at[x], hlow.at[x], hlow, 9)

    receive(10)
    gsum[...] = (gpack[core].astype(F32) + gcore[...].astype(F32)).astype(BF16)
    zy_all(lambda to: gsum.at[to], gz.at[zy], 12)
    sent(12, gz.at[pl.ds(0, 15)])
    gz[zy] = gsum[zy]

    receive(9)
    gradu = (adapter_scale * normalizer_scale) * dot(hlow[...].reshape(ROWS, 128), g_v[...], 0, 0)
    for c in range(2):
        upack[c] = packed_rows(gradu, c, 0)
    rcopy(upack.at[1 - core], ucore, 11, core_peer).start()
    sent(11, ucore)
    receive(11)
    usum[...] = (upack[core].astype(F32) + ucore[...].astype(F32)).astype(BF16)
    zy_all(lambda to: usum.at[to], uz.at[zy], 13)
    sent(13, uz.at[pl.ds(0, 15)])
    uz[zy] = usum[zy]

    for copy in loads[4:]:
        copy.wait()
    receive(12)
    gradient = unpack(jnp.sum(gz[...].astype(F32), axis=0), TD)
    new_p, new_m, new_v = adam(dp_v[...], dm_v[...], dv_v[...], gradient)
    fgat[r, pl.ds(0, PW)] = pack(new_p[:, :WCOLS], TW, PW)
    fgat[r, pl.ds(PW, PW)] = pack(new_p[:, WCOLS:], TW, PW)
    for j in FAR_FIRST:
        to = (yhi + j // 4) % 4 * 4 + (x + j % 4) % 4
        rcopy(fgat.at[r], fgat.at[r], 14, (l, to), roll_sem.at[r]).start()
    leaving.append((14, fgat.at[pl.ds(0, ROLL - 1)]))
    dpo[...] = new_p
    dmo[...] = new_m
    dvo[...] = new_v

    receive(13)
    gradient = unpack(jnp.sum(uz[...].astype(F32), axis=0), TU)
    new_p, new_m, new_v = adam(up_v[...], um_v[...], uv_v[...], gradient)
    unew[slot] = pack(new_p, TU, PU)
    zy_all(lambda to: unew.at[slot], unew.at[slot], 15)
    sent(15, unew.at[pl.ds(0, 15)])
    upo[...] = new_p
    umo[...] = new_m
    uvo[...] = new_v

    for j in (0,) + FAR_FIRST[::-1]:
        piece = (yhi + j // 4) % 4 * 4 + (x + j % 4) % 4
        if j:
            drain(fgat.at[piece], roll_sem.at[piece])
        near, far = fgat.at[piece, pl.ds(core * PW, PW)], fgat.at[piece, pl.ds((1 - core) * PW, PW)]
        rcopy(far, fbuf.at[l], 16, (2 * piece + 1 - core, r)).start()

        @pl.when(piece != zy)
        def _():
            rcopy(near, fbuf.at[l], 16, (2 * piece + core, r)).start()

        @pl.when(piece == zy)
        def _():
            pltpu.make_async_copy(near, fbuf.at[l], recv_sem.at[16]).start()

    arriving[16] = fbuf
    leaving.append((16, fbuf.at[pl.ds(0, LEARN - 1)]))

    receive(15)
    rcopy(unew.at[half], unew.at[half], 17, core_peer).start()
    sent(17, unew.at[pl.ds(0, 16)])
    receive(16)
    for k in range(0, TW, 4):
        packed = fbuf[:, OWN * k : OWN * k + 16].reshape(16, 2, 16, 128)
        for t, rows in enumerate(rank_rows((packed[:, 0], packed[:, 1]), min(4, TW - k))):
            dnew[:, 128 * (k + t) : 128 * (k + t) + 128] = rows
    receive(17)
    unpack_up(unew)
    finish()


def merge_kernel(w, umat, dnew, *refs):
    moved, wo_hbm, stored, wo_v, store_sem = refs[:6], refs[6], refs[7:13], refs[13], refs[14]
    stores = []

    def store(src, dst):
        copy = pltpu.make_async_copy(src, dst, store_sem.at[len(stores)])
        copy.start()
        stores.append(copy)

    for src, dst in zip(moved, stored):
        store(src, dst)
    for k in range(4):
        rows = slice(128 * k, 128 * k + 128)
        product = dot(umat[:, rows], dnew[...], 0, 0)
        wo_v[rows] = (w[rows].astype(F32) + adapter_scale * product).astype(BF16)
        store(wo_v.at[rows], wo_hbm.at[rows])
    for copy in stores:
        copy.wait()


def per_device(*args):
    down, up = (OWN, HID), (OWN, OUT)
    small = [down, down, down, up, up, up]
    hbm = pl.BlockSpec(memory_space=pltpu.HBM)
    vmem = pl.BlockSpec(memory_space=pltpu.VMEM)
    dma = pltpu.SemaphoreType.DMA

    def b(*shape):
        return pltpu.VMEM(shape, BF16)

    states = [jax.ShapeDtypeStruct(s, F32) for s in small]
    low = [b(NX, PART, 128) for _ in range(4)]
    made = pl.pallas_call(
        kernel,
        out_shape=[
            jax.ShapeDtypeStruct((OUT, WCOLS), BF16),
            jax.ShapeDtypeStruct((RANK, OUT), BF16),
            jax.ShapeDtypeStruct((RANK, WCOLS), BF16),
        ]
        + states,
        in_specs=[hbm] * 9,
        out_specs=[vmem] * 9,
        scratch_shapes=[b(ROWS, HID), b(ROWS, OUT)]
        + [pltpu.VMEM(s, F32) for s in small]
        + [b(LEARN, PU, 128), b(LEARN, PD, 128), b(RANK, HID)]
        + low
        + low
        + [b(2, 16, PD, 128), b(16, PD, 128), b(16, PD, 128), b(16, PD, 128)]
        + [b(2, 16, PU, 128), b(16, PU, 128), b(16, PU, 128), b(16, PU, 128), b(LEARN, PU, 128)]
        + [b(ROLL, 2 * PW, 128), b(LEARN, PW, 128)]
        + [dma((9,)), dma((18,)), dma((18,)), dma((ROLL,))],
        compiler_params=pltpu.CompilerParams(
            collective_id=0, has_side_effects=True, vmem_limit_bytes=40 * 2**20
        ),
        cost_estimate=pl.CostEstimate(flops=10**9, bytes_accessed=10**7, transcendentals=0),
        name="adapter_step",
    )(*(pltpu.with_memory_space_constraint(a, pltpu.HBM) for a in args))
    return tuple(
        pl.pallas_call(
            merge_kernel,
            out_shape=[jax.ShapeDtypeStruct((OUT, WCOLS), BF16)] + states,
            in_specs=[vmem] * 9,
            out_specs=[hbm] * 7,
            scratch_shapes=[b(OUT, WCOLS), dma((10,))],
            compiler_params=pltpu.CompilerParams(vmem_limit_bytes=20 * 2**20),
            cost_estimate=pl.CostEstimate(flops=10**8, bytes_accessed=2 * 10**6, transcendentals=0),
            name="merge",
        )(*made)
    )


def solution(mesh):
    return jax.shard_map(
        per_device,
        mesh=mesh,
        in_specs=(P("roll", "learn"),) + (P("learn", "roll"),) * 8,
        out_specs=(P("roll", "learn"),) + (P("learn", "roll"),) * 6,
        check_vma=False,
    )
```

```python
import math

import jax
import jax.numpy as jnp
from jax import lax
from jax.experimental import pallas as pl
from jax.experimental.pallas import tpu as pltpu
from jax.sharding import PartitionSpec as P

MESH = pl.DeviceIdType.MESH
BF16, F32 = jnp.bfloat16, jnp.float32

LEARN, ROLL, NX = 32, 16, 4
ZY_FAR_FIRST = tuple((dz, dp) for dz in (4, 3, 5, 2, 6, 1, 7) for dp in (1, 0)) + ((0, 1),)
RANK, TOKENS, OWN = 128, 20480, 4
ROWS, HID, OUT, WCOLS = 640, 1792, 512, 896
PART = ROWS // NX
TD, TU, TW = HID // 128, OUT // 128, WCOLS // 128
PD, PU, PW = 64, 16, 32

STEP = 20
adapter_scale = 2.0
learning_rate = 0.001
beta_one = 0.9
beta_two = 0.999
epsilon = 1e-08
weight_decay = 0.01


def adam(weights, moment_one, moment_two, gradient):
    one_next = beta_one * moment_one + (1.0 - beta_one) * gradient
    two_next = beta_two * moment_two + (1.0 - beta_two) * gradient * gradient
    corr_one = 1.0 - beta_one**STEP
    corr_two = 1.0 - beta_two**STEP
    update = one_next / corr_one / (jnp.sqrt(two_next / corr_two) + epsilon)
    return weights - learning_rate * (update + weight_decay * weights), one_next, two_next


def dot(a, b, ca, cb):
    return lax.dot_general(a, b, (((ca,), (cb,)), ((), ())), preferred_element_type=F32)


def pack(value, tiles, rows):
    parts = [value[:, 128 * t : 128 * t + 128] for t in range(tiles)]
    if rows > OWN * tiles:
        parts.append(jnp.zeros((rows - OWN * tiles, 128), value.dtype))
    return jnp.concatenate(parts, axis=0).astype(BF16)


def rank_rows(of_core, tiles):
    halves = [of_core[c].astype(F32) for c in range(2)]
    return [
        jnp.concatenate([h[:, OWN * t : OWN * t + OWN] for h in halves], axis=1)
        .reshape(RANK, 128)
        .astype(BF16)
        for t in range(tiles)
    ]


def packed_rows(grad, core, pad):
    tiles = [
        grad[:, 128 * t : 128 * t + 128].reshape(16, 2 * OWN, 128)[:, OWN * core : OWN * core + OWN]
        for t in range(grad.shape[1] // 128)
    ]
    if pad:
        tiles.append(jnp.zeros((16, pad, 128), F32))
    return jnp.concatenate(tiles, axis=1).astype(BF16)


def unpack(value, tiles):
    return jnp.concatenate([value[OWN * t : OWN * t + OWN] for t in range(tiles)], axis=1)


def kernel(
    w_hbm, x_hbm, g_hbm, dp_hbm, dm_hbm, dv_hbm, up_hbm, um_hbm, uv_hbm,
    w_v, umat, dnew, dpo, dmo, dvo, upo, umo, uvo,
    x_v, g_v, dp_v, dm_v, dv_v, up_v, um_v, uv_v,
    ubuf, dbuf, dmat,
    bpart, bx, bh, blow, hpart, hx, hh, hlow,
    gpack, gcore, gsum, gz, upack, ucore, usum, uz, unew, fgat, fbuf,
    load_sem, send_sem, recv_sem, roll_sem,
):
    l = lax.axis_index("learn")
    r = lax.axis_index("roll")
    zy, core = l // 2, l % 2
    yhi, x = r // 4, r % 4
    core_peer = (l + 1 - 2 * core, r)
    slot = core * 16 + zy

    loads = []
    for k, (src, dst) in enumerate(
        [(up_hbm, up_v), (dp_hbm, dp_v), (g_hbm, g_v), (x_hbm, x_v), (dm_hbm, dm_v), (dv_hbm, dv_v),
         (um_hbm, um_v), (uv_hbm, uv_v), (w_hbm, w_v)]
    ):
        loads.append(pltpu.make_async_copy(src, dst, load_sem.at[k]))
    load_up, load_dp, load_g, load_x = loads[:4]
    load_up.start()
    load_dp.start()

    barrier = pltpu.get_barrier_semaphore()

    def greet(to):
        pl.semaphore_signal(barrier, inc=1, device_id=to, device_id_type=MESH)

    def x_to(j):
        return yhi * 4 + (x + j) % 4

    def h_to(j):
        return ((yhi + j) % 4) * 4 + x

    def zy_to(dz, dp):
        return ((zy // 2 + dz) % 8) * 2 + (zy + dp) % 2

    for dz, dp in ZY_FAR_FIRST:
        greet((zy_to(dz, dp) * 2 + core, r))
    for j in (2, 1, 3):
        greet((l, h_to(j)))
        greet((l, x_to(j)))
    for dz, dp in ZY_FAR_FIRST:
        greet((zy_to(dz, dp) * 2 + 1 - core, r))
    greet(core_peer)
    for copy in loads[2:]:
        copy.start()

    load_up.wait()
    load_dp.wait()
    ubuf[slot] = pack(up_v[...], TU, PU)
    dbuf[slot] = pack(dp_v[...], TD, PD)
    pl.semaphore_wait(barrier, LEARN - 1 + 6)

    arriving, leaving = {}, []

    def rcopy(src, dst, k, to, sem=None):
        return pltpu.make_async_remote_copy(
            src_ref=src, dst_ref=dst, send_sem=send_sem.at[k],
            recv_sem=recv_sem.at[k] if sem is None else sem,
            device_id=to, device_id_type=MESH,
        )

    def drain(ref, sem):
        pltpu.make_async_copy(ref, ref, sem).wait()

    def sent(k, ref):
        arriving[k] = ref
        leaving.append((k, ref))

    def receive(k):
        drain(arriving.pop(k), recv_sem.at[k])

    def finish():
        for k in list(arriving):
            receive(k)
        for k, ref in leaving:
            drain(ref, send_sem.at[k])

    def zy_all(src_of, dst, k):
        for dz, dp in ZY_FAR_FIRST:
            to = zy_to(dz, dp)
            rcopy(src_of(to), dst, k, (to * 2 + core, r)).start()

    def x_all(src_of, dst, buf, k):
        for j in (2, 1, 3):
            rcopy(src_of((x + j) % 4), dst, k, (l, x_to(j))).start()
        sent(k, buf.at[pl.ds(0, 3)])

    def h_all(src, dst, buf, k):
        for j in (2, 1, 3):
            rcopy(src, dst, k, (l, h_to(j))).start()
        sent(k, buf.at[pl.ds(0, 3)])

    zy_all(lambda to: ubuf.at[slot], ubuf.at[slot], 0)
    sent(0, ubuf.at[pl.ds(0, 15)])
    zy_all(lambda to: dbuf.at[slot], dbuf.at[slot], 1)
    sent(1, dbuf.at[pl.ds(0, 15)])
    half = pl.ds(core * 16, 16)

    def unpack_up(buf):
        for t, rows in enumerate(rank_rows((buf[:16], buf[16:]), TU)):
            umat[:, 128 * t : 128 * t + 128] = rows

    def sum_four(buf):
        v = buf[...].astype(F32)
        return (v[0] + v[1]) + (v[2] + v[3])

    receive(0)
    rcopy(ubuf.at[half], ubuf.at[half], 2, core_peer).start()
    sent(2, ubuf.at[pl.ds(0, 16)])
    load_g.wait()
    receive(2)
    unpack_up(ubuf)
    bpart[...] = dot(g_v[...], umat[...], 1, 1).astype(BF16).reshape(NX, PART, 128)
    x_all(lambda to: bpart.at[to], bx.at[x], bx, 3)
    bx[x] = bpart[x]

    receive(1)
    rcopy(dbuf.at[half], dbuf.at[half], 4, core_peer).start()
    sent(4, dbuf.at[pl.ds(0, 16)])
    receive(3)
    bh[yhi] = sum_four(bx).astype(BF16)
    h_all(bh.at[yhi], bh.at[yhi], bh, 6)
    load_x.wait()
    receive(4)
    for k in range(0, TD, 4):
        packed = dbuf[:, OWN * k : OWN * k + 16]
        for t, rows in enumerate(rank_rows((packed[:16], packed[16:]), min(4, TD - k))):
            dmat[:, 128 * (k + t) : 128 * (k + t) + 128] = rows
    hpart[...] = dot(x_v[...], dmat[...], 1, 1).astype(BF16).reshape(NX, PART, 128)
    x_all(lambda to: hpart.at[to], hx.at[x], hx, 5)
    hx[x] = hpart[x]

    receive(5)
    hh[yhi] = sum_four(hx).astype(BF16)
    h_all(hh.at[yhi], hh.at[yhi], hh, 7)
    receive(6)
    blow[x] = (adapter_scale * sum_four(bh)).astype(BF16)
    x_all(lambda to: blow.at[x], blow.at[x], blow, 8)

    normalizer_scale = 1.0 / math.sqrt(TOKENS)
    receive(8)
    low = blow[...].reshape(ROWS, 128)
    for k in range(0, TD, 4):
        tiles = min(4, TD - k)
        grad = normalizer_scale * dot(low, x_v[:, 128 * k : 128 * (k + tiles)], 0, 0)
        for c in range(2):
            gpack[c, :, OWN * k : OWN * k + 16] = packed_rows(grad, c, 16 - OWN * tiles)
    rcopy(gpack.at[1 - core], gcore, 10, core_peer).start()
    sent(10, gcore)

    receive(10)
    gsum[...] = (gpack[core].astype(F32) + gcore[...].astype(F32)).astype(BF16)
    zy_all(lambda to: gsum.at[to], gz.at[zy], 12)
    sent(12, gz.at[pl.ds(0, 15)])
    gz[zy] = gsum[zy]

    receive(7)
    hlow[x] = sum_four(hh).astype(BF16)
    x_all(lambda to: hlow.at[x], hlow.at[x], hlow, 9)

    receive(9)
    gradu = (adapter_scale * normalizer_scale) * dot(hlow[...].reshape(ROWS, 128), g_v[...], 0, 0)
    for c in range(2):
        upack[c] = packed_rows(gradu, c, 0)
    rcopy(upack.at[1 - core], ucore, 11, core_peer).start()
    sent(11, ucore)
    receive(11)
    usum[...] = (upack[core].astype(F32) + ucore[...].astype(F32)).astype(BF16)
    zy_all(lambda to: usum.at[to], uz.at[zy], 13)
    sent(13, uz.at[pl.ds(0, 15)])
    uz[zy] = usum[zy]

    for copy in loads[4:]:
        copy.wait()
    receive(12)
    gradient = unpack(jnp.sum(gz[...].astype(F32), axis=0), TD)
    new_p, new_m, new_v = adam(dp_v[...], dm_v[...], dv_v[...], gradient)
    fgat[r, pl.ds(0, PW)] = pack(new_p[:, :WCOLS], TW, PW)
    fgat[r, pl.ds(PW, PW)] = pack(new_p[:, WCOLS:], TW, PW)

    def pass_on(piece, to):
        rcopy(fgat.at[piece], fgat.at[piece], 14, (l, to), roll_sem.at[piece]).start()

    def arrived(j):
        piece = (yhi + j // 4) % 4 * 4 + (x + j % 4) % 4
        if j:
            drain(fgat.at[piece], roll_sem.at[piece])
        return piece

    for j in (2, 1, 3):
        pass_on(r, h_to(j))
    for j in (2, 1, 3):
        pass_on(r, x_to(j))
    leaving.append((14, fgat.at[pl.ds(0, ROLL - 1)]))
    dpo[...] = new_p
    dmo[...] = new_m
    dvo[...] = new_v

    def forward(piece):
        near, far = fgat.at[piece, pl.ds(core * PW, PW)], fgat.at[piece, pl.ds((1 - core) * PW, PW)]
        rcopy(far, fbuf.at[l], 16, (2 * piece + 1 - core, r)).start()

        @pl.when(piece != zy)
        def _():
            rcopy(near, fbuf.at[l], 16, (2 * piece + core, r)).start()

        @pl.when(piece == zy)
        def _():
            pltpu.make_async_copy(near, fbuf.at[l], recv_sem.at[16]).start()

    receive(13)
    gradient = unpack(jnp.sum(uz[...].astype(F32), axis=0), TU)
    new_p, new_m, new_v = adam(up_v[...], um_v[...], uv_v[...], gradient)
    unew[slot] = pack(new_p, TU, PU)
    zy_all(lambda to: unew.at[slot], unew.at[slot], 15)
    sent(15, unew.at[pl.ds(0, 15)])
    upo[...] = new_p
    umo[...] = new_m
    uvo[...] = new_v

    for j in (0, 1, 3, 2):
        forward(arrived(j))
    for j in (4, 12, 8):
        piece = arrived(j)
        for k in (2, 1, 3):
            pass_on(piece, x_to(k))
        forward(piece)
    for j in (5, 7, 13, 15, 6, 14, 9, 11, 10):
        forward(arrived(j))
    arriving[16] = fbuf
    leaving.append((16, fbuf.at[pl.ds(0, LEARN - 1)]))

    receive(15)
    rcopy(unew.at[half], unew.at[half], 17, core_peer).start()
    sent(17, unew.at[pl.ds(0, 16)])
    receive(16)
    for k in range(0, TW, 4):
        packed = fbuf[:, OWN * k : OWN * k + 16].reshape(16, 2, 16, 128)
        for t, rows in enumerate(rank_rows((packed[:, 0], packed[:, 1]), min(4, TW - k))):
            dnew[:, 128 * (k + t) : 128 * (k + t) + 128] = rows
    receive(17)
    unpack_up(unew)
    finish()


def merge_kernel(w, umat, dnew, *refs):
    moved, wo_hbm, stored, wo_v, store_sem = refs[:6], refs[6], refs[7:13], refs[13], refs[14]
    stores = []

    def store(src, dst):
        copy = pltpu.make_async_copy(src, dst, store_sem.at[len(stores)])
        copy.start()
        stores.append(copy)

    for src, dst in zip(moved, stored):
        store(src, dst)
    for k in range(4):
        rows = slice(128 * k, 128 * k + 128)
        product = dot(umat[:, rows], dnew[...], 0, 0)
        wo_v[rows] = (w[rows].astype(F32) + adapter_scale * product).astype(BF16)
        store(wo_v.at[rows], wo_hbm.at[rows])
    for copy in stores:
        copy.wait()


def per_device(*args):
    down, up = (OWN, HID), (OWN, OUT)
    small = [down, down, down, up, up, up]
    hbm = pl.BlockSpec(memory_space=pltpu.HBM)
    vmem = pl.BlockSpec(memory_space=pltpu.VMEM)
    dma = pltpu.SemaphoreType.DMA

    def b(*shape):
        return pltpu.VMEM(shape, BF16)

    states = [jax.ShapeDtypeStruct(s, F32) for s in small]
    low = [b(NX, PART, 128) for _ in range(4)]
    made = pl.pallas_call(
        kernel,
        out_shape=[
            jax.ShapeDtypeStruct((OUT, WCOLS), BF16),
            jax.ShapeDtypeStruct((RANK, OUT), BF16),
            jax.ShapeDtypeStruct((RANK, WCOLS), BF16),
        ]
        + states,
        in_specs=[hbm] * 9,
        out_specs=[vmem] * 9,
        scratch_shapes=[b(ROWS, HID), b(ROWS, OUT)]
        + [pltpu.VMEM(s, F32) for s in small]
        + [b(LEARN, PU, 128), b(LEARN, PD, 128), b(RANK, HID)]
        + low
        + low
        + [b(2, 16, PD, 128), b(16, PD, 128), b(16, PD, 128), b(16, PD, 128)]
        + [b(2, 16, PU, 128), b(16, PU, 128), b(16, PU, 128), b(16, PU, 128), b(LEARN, PU, 128)]
        + [b(ROLL, 2 * PW, 128), b(LEARN, PW, 128)]
        + [dma((9,)), dma((18,)), dma((18,)), dma((ROLL,))],
        compiler_params=pltpu.CompilerParams(
            collective_id=0, has_side_effects=True, vmem_limit_bytes=40 * 2**20
        ),
        cost_estimate=pl.CostEstimate(flops=10**9, bytes_accessed=10**7, transcendentals=0),
        name="adapter_step",
    )(*(pltpu.with_memory_space_constraint(a, pltpu.HBM) for a in args))
    return tuple(
        pl.pallas_call(
            merge_kernel,
            out_shape=[jax.ShapeDtypeStruct((OUT, WCOLS), BF16)] + states,
            in_specs=[vmem] * 9,
            out_specs=[hbm] * 7,
            scratch_shapes=[b(OUT, WCOLS), dma((10,))],
            compiler_params=pltpu.CompilerParams(vmem_limit_bytes=20 * 2**20),
            cost_estimate=pl.CostEstimate(flops=10**8, bytes_accessed=2 * 10**6, transcendentals=0),
            name="merge",
        )(*made)
    )


def solution(mesh):
    return jax.shard_map(
        per_device,
        mesh=mesh,
        in_specs=(P("roll", "learn"),) + (P("learn", "roll"),) * 8,
        out_specs=(P("roll", "learn"),) + (P("learn", "roll"),) * 6,
        check_vma=False,
    )
```

```python
import math

import jax
import jax.numpy as jnp
from jax import lax
from jax.experimental import pallas as pl
from jax.experimental.pallas import tpu as pltpu
from jax.sharding import PartitionSpec as P

MESH = pl.DeviceIdType.MESH
BF16, F32 = jnp.bfloat16, jnp.float32

LEARN, ROLL, NX = 32, 16, 4
ZY_FAR_FIRST = tuple((dz, dp) for dz in (4, 3, 5, 2, 6, 1, 7) for dp in (1, 0)) + ((0, 1),)
RANK, TOKENS, OWN = 128, 20480, 4
ROWS, HID, OUT, WCOLS = 640, 1792, 512, 896
PART = ROWS // NX
TD, TU, TW = HID // 128, OUT // 128, WCOLS // 128
PD, PU, PW = 64, 16, 32

STEP = 20
adapter_scale = 2.0
learning_rate = 0.001
beta_one = 0.9
beta_two = 0.999
epsilon = 1e-08
weight_decay = 0.01


def adam(weights, moment_one, moment_two, gradient):
    one_next = beta_one * moment_one + (1.0 - beta_one) * gradient
    two_next = beta_two * moment_two + (1.0 - beta_two) * gradient * gradient
    corr_one = 1.0 - beta_one**STEP
    corr_two = 1.0 - beta_two**STEP
    update = one_next / corr_one / (jnp.sqrt(two_next / corr_two) + epsilon)
    return weights - learning_rate * (update + weight_decay * weights), one_next, two_next


def dot(a, b, ca, cb):
    return lax.dot_general(a, b, (((ca,), (cb,)), ((), ())), preferred_element_type=F32)


def pack(value, tiles, rows):
    parts = [value[:, 128 * t : 128 * t + 128] for t in range(tiles)]
    if rows > OWN * tiles:
        parts.append(jnp.zeros((rows - OWN * tiles, 128), value.dtype))
    return jnp.concatenate(parts, axis=0).astype(BF16)


def rank_rows(of_core, tiles):
    halves = [of_core[c].astype(F32) for c in range(2)]
    return [
        jnp.concatenate([h[:, OWN * t : OWN * t + OWN] for h in halves], axis=1)
        .reshape(RANK, 128)
        .astype(BF16)
        for t in range(tiles)
    ]


def packed_rows(grad, core, pad):
    tiles = [
        grad[:, 128 * t : 128 * t + 128].reshape(16, 2 * OWN, 128)[:, OWN * core : OWN * core + OWN]
        for t in range(grad.shape[1] // 128)
    ]
    if pad:
        tiles.append(jnp.zeros((16, pad, 128), F32))
    return jnp.concatenate(tiles, axis=1).astype(BF16)


def unpack(value, tiles):
    return jnp.concatenate([value[OWN * t : OWN * t + OWN] for t in range(tiles)], axis=1)


def kernel(
    w_hbm, x_hbm, g_hbm, dp_hbm, dm_hbm, dv_hbm, up_hbm, um_hbm, uv_hbm,
    w_v, umat, dnew, dpo, dmo, dvo, upo, umo, uvo,
    x_v, g_v, dp_v, dm_v, dv_v, up_v, um_v, uv_v,
    ubuf, dbuf, dmat,
    bpart, bx, bh, blow, hpart, hx, hh, hlow,
    gpack, gcore, gsum, gz, upack, ucore, usum, uz, unew, fgat, fbuf,
    load_sem, send_sem, recv_sem, roll_sem,
):
    l = lax.axis_index("learn")
    r = lax.axis_index("roll")
    zy, core = l // 2, l % 2
    yhi, x = r // 4, r % 4
    core_peer = (l + 1 - 2 * core, r)
    slot = core * 16 + zy

    loads = []
    for k, (src, dst) in enumerate(
        [(up_hbm, up_v), (dp_hbm, dp_v), (g_hbm, g_v), (x_hbm, x_v), (dm_hbm, dm_v), (dv_hbm, dv_v),
         (um_hbm, um_v), (uv_hbm, uv_v), (w_hbm, w_v)]
    ):
        loads.append(pltpu.make_async_copy(src, dst, load_sem.at[k]))
    load_up, load_dp, load_g, load_x = loads[:4]
    load_up.start()
    load_dp.start()

    barrier = pltpu.get_barrier_semaphore()

    def greet(to):
        pl.semaphore_signal(barrier, inc=1, device_id=to, device_id_type=MESH)

    def x_to(j):
        return yhi * 4 + (x + j) % 4

    def h_to(j):
        return ((yhi + j) % 4) * 4 + x

    def zy_to(dz, dp):
        return ((zy // 2 + dz) % 8) * 2 + (zy + dp) % 2

    for dz, dp in ZY_FAR_FIRST:
        greet((zy_to(dz, dp) * 2 + core, r))
    for j in (2, 1, 3):
        greet((l, h_to(j)))
        greet((l, x_to(j)))
    for dz, dp in ZY_FAR_FIRST:
        greet((zy_to(dz, dp) * 2 + 1 - core, r))
    greet(core_peer)
    for copy in loads[2:]:
        copy.start()

    load_up.wait()
    load_dp.wait()
    ubuf[slot] = pack(up_v[...], TU, PU)
    dbuf[slot] = pack(dp_v[...], TD, PD)
    pl.semaphore_wait(barrier, LEARN - 1 + 6)

    arriving, leaving = {}, []

    def rcopy(src, dst, k, to, sem=None):
        return pltpu.make_async_remote_copy(
            src_ref=src, dst_ref=dst, send_sem=send_sem.at[k],
            recv_sem=recv_sem.at[k] if sem is None else sem,
            device_id=to, device_id_type=MESH,
        )

    def drain(ref, sem):
        pltpu.make_async_copy(ref, ref, sem).wait()

    def sent(k, ref):
        arriving[k] = ref
        leaving.append((k, ref))

    def receive(k):
        drain(arriving.pop(k), recv_sem.at[k])

    def finish():
        for k in list(arriving):
            receive(k)
        for k, ref in leaving:
            drain(ref, send_sem.at[k])

    def zy_all(src_of, dst, k):
        for dz, dp in ZY_FAR_FIRST:
            to = zy_to(dz, dp)
            rcopy(src_of(to), dst, k, (to * 2 + core, r)).start()

    def part_rows(left, right, part, landing, k):
        for j in (2, 1, 3, 0):
            to = (x + j) % 4
            rows = left[pl.ds(pl.multiple_of(to * PART, PART), PART)]
            if j:
                part[to] = dot(rows, right[...], 1, 1).astype(BF16)
                rcopy(part.at[to], landing.at[x], k, (l, x_to(j))).start()
            else:
                landing[to] = dot(rows, right[...], 1, 1).astype(BF16)
        sent(k, landing.at[pl.ds(0, 3)])

    def x_all(src_of, dst, buf, k):
        for j in (2, 1, 3):
            rcopy(src_of((x + j) % 4), dst, k, (l, x_to(j))).start()
        sent(k, buf.at[pl.ds(0, 3)])

    def h_all(src, dst, buf, k):
        for j in (2, 1, 3):
            rcopy(src, dst, k, (l, h_to(j))).start()
        sent(k, buf.at[pl.ds(0, 3)])

    for dz, dp in ZY_FAR_FIRST:
        for to_core in (core, 1 - core):
            rcopy(ubuf.at[slot], ubuf.at[slot], 0, (zy_to(dz, dp) * 2 + to_core, r)).start()
    rcopy(ubuf.at[slot], ubuf.at[slot], 0, core_peer).start()
    sent(0, ubuf.at[pl.ds(0, LEARN - 1)])
    zy_all(lambda to: dbuf.at[slot], dbuf.at[slot], 1)
    sent(1, dbuf.at[pl.ds(0, 15)])
    half = pl.ds(core * 16, 16)

    def unpack_up(buf):
        for t, rows in enumerate(rank_rows((buf[:16], buf[16:]), TU)):
            umat[:, 128 * t : 128 * t + 128] = rows

    def sum_four(buf):
        v = buf[...].astype(F32)
        return (v[0] + v[1]) + (v[2] + v[3])

    load_g.wait()
    receive(0)
    unpack_up(ubuf)
    part_rows(g_v, umat, bpart, bx, 3)

    receive(1)
    rcopy(dbuf.at[half], dbuf.at[half], 4, core_peer).start()
    sent(4, dbuf.at[pl.ds(0, 16)])
    receive(3)
    bh[yhi] = sum_four(bx).astype(BF16)
    h_all(bh.at[yhi], bh.at[yhi], bh, 6)
    load_x.wait()
    receive(4)
    for k in range(0, TD, 4):
        packed = dbuf[:, OWN * k : OWN * k + 16]
        for t, rows in enumerate(rank_rows((packed[:16], packed[16:]), min(4, TD - k))):
            dmat[:, 128 * (k + t) : 128 * (k + t) + 128] = rows
    part_rows(x_v, dmat, hpart, hx, 5)

    receive(5)
    hh[yhi] = sum_four(hx).astype(BF16)
    h_all(hh.at[yhi], hh.at[yhi], hh, 7)
    receive(6)
    blow[x] = (adapter_scale * sum_four(bh)).astype(BF16)
    x_all(lambda to: blow.at[x], blow.at[x], blow, 8)

    normalizer_scale = 1.0 / math.sqrt(TOKENS)
    receive(8)
    low = blow[...].reshape(ROWS, 128)
    for k in range(0, TD, 4):
        tiles = min(4, TD - k)
        grad = normalizer_scale * dot(low, x_v[:, 128 * k : 128 * (k + tiles)], 0, 0)
        for c in range(2):
            gpack[c, :, OWN * k : OWN * k + 16] = packed_rows(grad, c, 16 - OWN * tiles)
    rcopy(gpack.at[1 - core], gcore, 10, core_peer).start()
    sent(10, gcore)

    receive(10)
    gsum[...] = (gpack[core].astype(F32) + gcore[...].astype(F32)).astype(BF16)
    zy_all(lambda to: gsum.at[to], gz.at[zy], 12)
    sent(12, gz.at[pl.ds(0, 15)])
    gz[zy] = gsum[zy]

    receive(7)
    hlow[x] = sum_four(hh).astype(BF16)
    x_all(lambda to: hlow.at[x], hlow.at[x], hlow, 9)

    receive(9)
    gradu = (adapter_scale * normalizer_scale) * dot(hlow[...].reshape(ROWS, 128), g_v[...], 0, 0)
    for c in range(2):
        upack[c] = packed_rows(gradu, c, 0)
    rcopy(upack.at[1 - core], ucore, 11, core_peer).start()
    sent(11, ucore)
    receive(11)
    usum[...] = (upack[core].astype(F32) + ucore[...].astype(F32)).astype(BF16)
    zy_all(lambda to: usum.at[to], uz.at[zy], 13)
    sent(13, uz.at[pl.ds(0, 15)])
    uz[zy] = usum[zy]

    for copy in loads[4:]:
        copy.wait()
    receive(12)
    gradient = unpack(jnp.sum(gz[...].astype(F32), axis=0), TD)
    new_p, new_m, new_v = adam(dp_v[...], dm_v[...], dv_v[...], gradient)
    fgat[r, pl.ds(0, PW)] = pack(new_p[:, :WCOLS], TW, PW)
    fgat[r, pl.ds(PW, PW)] = pack(new_p[:, WCOLS:], TW, PW)

    def pass_on(piece, to):
        rcopy(fgat.at[piece], fgat.at[piece], 14, (l, to), roll_sem.at[piece]).start()

    def arrived(j):
        piece = (yhi + j // 4) % 4 * 4 + (x + j % 4) % 4
        if j:
            drain(fgat.at[piece], roll_sem.at[piece])
        return piece

    for j in (2, 1, 3):
        pass_on(r, h_to(j))
    for j in (2, 1, 3):
        pass_on(r, x_to(j))
    leaving.append((14, fgat.at[pl.ds(0, ROLL - 1)]))
    dpo[...] = new_p
    dmo[...] = new_m
    dvo[...] = new_v

    def forward(piece):
        near, far = fgat.at[piece, pl.ds(core * PW, PW)], fgat.at[piece, pl.ds((1 - core) * PW, PW)]
        rcopy(far, fbuf.at[l], 16, (2 * piece + 1 - core, r)).start()

        @pl.when(piece != zy)
        def _():
            rcopy(near, fbuf.at[l], 16, (2 * piece + core, r)).start()

        @pl.when(piece == zy)
        def _():
            pltpu.make_async_copy(near, fbuf.at[l], recv_sem.at[16]).start()

    receive(13)
    gradient = unpack(jnp.sum(uz[...].astype(F32), axis=0), TU)
    new_p, new_m, new_v = adam(up_v[...], um_v[...], uv_v[...], gradient)
    unew[slot] = pack(new_p, TU, PU)
    zy_all(lambda to: unew.at[slot], unew.at[slot], 15)
    sent(15, unew.at[pl.ds(0, 15)])
    upo[...] = new_p
    umo[...] = new_m
    uvo[...] = new_v

    for j in (0, 1, 3, 2):
        forward(arrived(j))
    for j in (4, 12, 8):
        piece = arrived(j)
        for k in (2, 1, 3):
            pass_on(piece, x_to(k))
        forward(piece)
    for j in (5, 7, 13, 15, 6, 14, 9, 11, 10):
        forward(arrived(j))
    arriving[16] = fbuf
    leaving.append((16, fbuf.at[pl.ds(0, LEARN - 1)]))

    receive(15)
    rcopy(unew.at[half], unew.at[half], 17, core_peer).start()
    sent(17, unew.at[pl.ds(0, 16)])
    receive(16)
    for k in range(0, TW, 4):
        packed = fbuf[:, OWN * k : OWN * k + 16].reshape(16, 2, 16, 128)
        for t, rows in enumerate(rank_rows((packed[:, 0], packed[:, 1]), min(4, TW - k))):
            dnew[:, 128 * (k + t) : 128 * (k + t) + 128] = rows
    receive(17)
    unpack_up(unew)
    finish()


def merge_kernel(w, umat, dnew, *refs):
    moved, wo_hbm, stored, wo_v, store_sem = refs[:6], refs[6], refs[7:13], refs[13], refs[14]
    stores = []

    def store(src, dst):
        copy = pltpu.make_async_copy(src, dst, store_sem.at[len(stores)])
        copy.start()
        stores.append(copy)

    for src, dst in zip(moved, stored):
        store(src, dst)
    for k in range(4):
        rows = slice(128 * k, 128 * k + 128)
        product = dot(umat[:, rows], dnew[...], 0, 0)
        wo_v[rows] = (w[rows].astype(F32) + adapter_scale * product).astype(BF16)
        store(wo_v.at[rows], wo_hbm.at[rows])
    for copy in stores:
        copy.wait()


def per_device(*args):
    down, up = (OWN, HID), (OWN, OUT)
    small = [down, down, down, up, up, up]
    hbm = pl.BlockSpec(memory_space=pltpu.HBM)
    vmem = pl.BlockSpec(memory_space=pltpu.VMEM)
    dma = pltpu.SemaphoreType.DMA

    def b(*shape):
        return pltpu.VMEM(shape, BF16)

    states = [jax.ShapeDtypeStruct(s, F32) for s in small]
    low = [b(NX, PART, 128) for _ in range(4)]
    made = pl.pallas_call(
        kernel,
        out_shape=[
            jax.ShapeDtypeStruct((OUT, WCOLS), BF16),
            jax.ShapeDtypeStruct((RANK, OUT), BF16),
            jax.ShapeDtypeStruct((RANK, WCOLS), BF16),
        ]
        + states,
        in_specs=[hbm] * 9,
        out_specs=[vmem] * 9,
        scratch_shapes=[b(ROWS, HID), b(ROWS, OUT)]
        + [pltpu.VMEM(s, F32) for s in small]
        + [b(LEARN, PU, 128), b(LEARN, PD, 128), b(RANK, HID)]
        + low
        + low
        + [b(2, 16, PD, 128), b(16, PD, 128), b(16, PD, 128), b(16, PD, 128)]
        + [b(2, 16, PU, 128), b(16, PU, 128), b(16, PU, 128), b(16, PU, 128), b(LEARN, PU, 128)]
        + [b(ROLL, 2 * PW, 128), b(LEARN, PW, 128)]
        + [dma((9,)), dma((18,)), dma((18,)), dma((ROLL,))],
        compiler_params=pltpu.CompilerParams(
            collective_id=0, has_side_effects=True, vmem_limit_bytes=40 * 2**20
        ),
        cost_estimate=pl.CostEstimate(flops=10**9, bytes_accessed=10**7, transcendentals=0),
        name="adapter_step",
    )(*(pltpu.with_memory_space_constraint(a, pltpu.HBM) for a in args))
    return tuple(
        pl.pallas_call(
            merge_kernel,
            out_shape=[jax.ShapeDtypeStruct((OUT, WCOLS), BF16)] + states,
            in_specs=[vmem] * 9,
            out_specs=[hbm] * 7,
            scratch_shapes=[b(OUT, WCOLS), dma((10,))],
            compiler_params=pltpu.CompilerParams(vmem_limit_bytes=20 * 2**20),
            cost_estimate=pl.CostEstimate(flops=10**8, bytes_accessed=2 * 10**6, transcendentals=0),
            name="merge",
        )(*made)
    )


def solution(mesh):
    return jax.shard_map(
        per_device,
        mesh=mesh,
        in_specs=(P("roll", "learn"),) + (P("learn", "roll"),) * 8,
        out_specs=(P("roll", "learn"),) + (P("learn", "roll"),) * 6,
        check_vma=False,
    )
```

```python
import math

import jax
import jax.numpy as jnp
from jax import lax
from jax.experimental import pallas as pl
from jax.experimental.pallas import tpu as pltpu
from jax.sharding import PartitionSpec as P

MESH = pl.DeviceIdType.MESH
BF16, F32 = jnp.bfloat16, jnp.float32

LEARN, ROLL, NX = 32, 16, 4
ZY_FAR_FIRST = tuple((dz, dp) for dz in (4, 3, 5, 2, 6, 1, 7) for dp in (1, 0)) + ((0, 1),)
RANK, TOKENS, OWN = 128, 20480, 4
ROWS, HID, OUT, WCOLS = 640, 1792, 512, 896
PART = ROWS // NX
TD, TU, TW = HID // 128, OUT // 128, WCOLS // 128
PD, PU, PW = 64, 16, 32

STEP = 20
adapter_scale = 2.0
learning_rate = 0.001
beta_one = 0.9
beta_two = 0.999
epsilon = 1e-08
weight_decay = 0.01


def adam(weights, moment_one, moment_two, gradient):
    one_next = beta_one * moment_one + (1.0 - beta_one) * gradient
    two_next = beta_two * moment_two + (1.0 - beta_two) * gradient * gradient
    corr_one = 1.0 - beta_one**STEP
    corr_two = 1.0 - beta_two**STEP
    update = one_next / corr_one / (jnp.sqrt(two_next / corr_two) + epsilon)
    return weights - learning_rate * (update + weight_decay * weights), one_next, two_next


def dot(a, b, ca, cb):
    return lax.dot_general(a, b, (((ca,), (cb,)), ((), ())), preferred_element_type=F32)


def pack(value, tiles, rows):
    parts = [value[:, 128 * t : 128 * t + 128] for t in range(tiles)]
    if rows > OWN * tiles:
        parts.append(jnp.zeros((rows - OWN * tiles, 128), value.dtype))
    return jnp.concatenate(parts, axis=0).astype(BF16)


def rank_rows(of_core, tiles):
    halves = [of_core[c].astype(F32) for c in range(2)]
    return [
        jnp.concatenate([h[:, OWN * t : OWN * t + OWN] for h in halves], axis=1)
        .reshape(RANK, 128)
        .astype(BF16)
        for t in range(tiles)
    ]


def packed_rows(grad, core, pad):
    tiles = [
        grad[:, 128 * t : 128 * t + 128].reshape(16, 2 * OWN, 128)[:, OWN * core : OWN * core + OWN]
        for t in range(grad.shape[1] // 128)
    ]
    if pad:
        tiles.append(jnp.zeros((16, pad, 128), F32))
    return jnp.concatenate(tiles, axis=1).astype(BF16)


def unpack(value, tiles):
    return jnp.concatenate([value[OWN * t : OWN * t + OWN] for t in range(tiles)], axis=1)


def kernel(
    w_hbm, x_hbm, g_hbm, dp_hbm, dm_hbm, dv_hbm, up_hbm, um_hbm, uv_hbm,
    w_v, umat, dnew, dpo, dmo, dvo, upo, umo, uvo,
    x_v, g_v, dp_v, dm_v, dv_v, up_v, um_v, uv_v,
    ubuf, dbuf, dmat,
    bpart, bx, bh, blow, hpart, hx, hh, hlow,
    gpack, gcore, gsum, gz, upack, ucore, usum, uz, unew, fgat, fbuf,
    load_sem, send_sem, recv_sem, roll_sem,
):
    l = lax.axis_index("learn")
    r = lax.axis_index("roll")
    zy, core = l // 2, l % 2
    yhi, x = r // 4, r % 4
    core_peer = (l + 1 - 2 * core, r)
    slot = core * 16 + zy

    loads = []
    for k, (src, dst) in enumerate(
        [(up_hbm, up_v), (dp_hbm, dp_v), (g_hbm, g_v), (x_hbm, x_v), (dm_hbm, dm_v), (dv_hbm, dv_v),
         (um_hbm, um_v), (uv_hbm, uv_v), (w_hbm, w_v)]
    ):
        loads.append(pltpu.make_async_copy(src, dst, load_sem.at[k]))
    load_up, load_dp, load_g, load_x = loads[:4]
    load_up.start()
    load_dp.start()

    barrier = pltpu.get_barrier_semaphore()

    def greet(to):
        pl.semaphore_signal(barrier, inc=1, device_id=to, device_id_type=MESH)

    def x_to(j):
        return yhi * 4 + (x + j) % 4

    def h_to(j):
        return ((yhi + j) % 4) * 4 + x

    def zy_to(dz, dp):
        return ((zy // 2 + dz) % 8) * 2 + (zy + dp) % 2

    for dz, dp in ZY_FAR_FIRST:
        greet((zy_to(dz, dp) * 2 + core, r))
    for j in (2, 1, 3):
        greet((l, h_to(j)))
        greet((l, x_to(j)))
    for dz, dp in ZY_FAR_FIRST:
        greet((zy_to(dz, dp) * 2 + 1 - core, r))
    greet(core_peer)
    for copy in loads[2:]:
        copy.start()

    load_up.wait()
    load_dp.wait()
    ubuf[slot] = pack(up_v[...], TU, PU)
    dbuf[slot] = pack(dp_v[...], TD, PD)
    pl.semaphore_wait(barrier, LEARN - 1 + 6)

    arriving, leaving = {}, []

    def rcopy(src, dst, k, to, sem=None):
        return pltpu.make_async_remote_copy(
            src_ref=src, dst_ref=dst, send_sem=send_sem.at[k],
            recv_sem=recv_sem.at[k] if sem is None else sem,
            device_id=to, device_id_type=MESH,
        )

    def drain(ref, sem):
        pltpu.make_async_copy(ref, ref, sem).wait()

    def sent(k, ref):
        arriving[k] = ref
        leaving.append((k, ref))

    def receive(k):
        drain(arriving.pop(k), recv_sem.at[k])

    def finish():
        for k in list(arriving):
            receive(k)
        for k, ref in leaving:
            drain(ref, send_sem.at[k])

    def zy_all(src_of, dst, k):
        for dz, dp in ZY_FAR_FIRST:
            to = zy_to(dz, dp)
            rcopy(src_of(to), dst, k, (to * 2 + core, r)).start()

    def part_rows(left, right, part, landing, k):
        for j in (2, 1, 3, 0):
            to = (x + j) % 4
            rows = left[pl.ds(pl.multiple_of(to * PART, PART), PART)]
            if j:
                part[to] = dot(rows, right[...], 1, 1).astype(BF16)
                rcopy(part.at[to], landing.at[x], k, (l, x_to(j))).start()
            else:
                landing[to] = dot(rows, right[...], 1, 1).astype(BF16)
        sent(k, landing.at[pl.ds(0, 3)])

    def x_all(src_of, dst, buf, k):
        for j in (2, 1, 3):
            rcopy(src_of((x + j) % 4), dst, k, (l, x_to(j))).start()
        sent(k, buf.at[pl.ds(0, 3)])

    def h_all(src, dst, buf, k):
        for j in (2, 1, 3):
            rcopy(src, dst, k, (l, h_to(j))).start()
        sent(k, buf.at[pl.ds(0, 3)])

    for dz, dp in ZY_FAR_FIRST:
        for to_core in (core, 1 - core):
            rcopy(ubuf.at[slot], ubuf.at[slot], 0, (zy_to(dz, dp) * 2 + to_core, r)).start()
    rcopy(ubuf.at[slot], ubuf.at[slot], 0, core_peer).start()
    sent(0, ubuf.at[pl.ds(0, LEARN - 1)])
    zy_all(lambda to: dbuf.at[slot], dbuf.at[slot], 1)
    sent(1, dbuf.at[pl.ds(0, 15)])
    half = pl.ds(core * 16, 16)

    def unpack_up(buf):
        for t, rows in enumerate(rank_rows((buf[:16], buf[16:]), TU)):
            umat[:, 128 * t : 128 * t + 128] = rows

    def sum_four(buf):
        v = buf[...].astype(F32)
        return (v[0] + v[1]) + (v[2] + v[3])

    load_g.wait()
    receive(0)
    unpack_up(ubuf)
    part_rows(g_v, umat, bpart, bx, 3)

    receive(1)
    rcopy(dbuf.at[half], dbuf.at[half], 4, core_peer).start()
    sent(4, dbuf.at[pl.ds(0, 16)])
    receive(3)
    bh[yhi] = sum_four(bx).astype(BF16)
    h_all(bh.at[yhi], bh.at[yhi], bh, 6)
    load_x.wait()
    receive(4)
    for k in range(0, TD, 4):
        packed = dbuf[:, OWN * k : OWN * k + 16]
        for t, rows in enumerate(rank_rows((packed[:16], packed[16:]), min(4, TD - k))):
            dmat[:, 128 * (k + t) : 128 * (k + t) + 128] = rows
    part_rows(x_v, dmat, hpart, hx, 5)

    receive(5)
    hh[yhi] = sum_four(hx).astype(BF16)
    h_all(hh.at[yhi], hh.at[yhi], hh, 7)
    receive(6)
    blow[x] = (adapter_scale * sum_four(bh)).astype(BF16)
    x_all(lambda to: blow.at[x], blow.at[x], blow, 8)

    normalizer_scale = 1.0 / math.sqrt(TOKENS)
    receive(8)
    low = blow[...].reshape(ROWS, 128)
    for k in range(0, TD, 4):
        tiles = min(4, TD - k)
        grad = normalizer_scale * dot(low, x_v[:, 128 * k : 128 * (k + tiles)], 0, 0)
        for c in range(2):
            gpack[c, :, OWN * k : OWN * k + 16] = packed_rows(grad, c, 16 - OWN * tiles)
    rcopy(gpack.at[1 - core], gcore, 10, core_peer).start()
    sent(10, gcore)

    receive(10)
    gsum[...] = (gpack[core].astype(F32) + gcore[...].astype(F32)).astype(BF16)
    zy_all(lambda to: gsum.at[to], gz.at[zy], 12)
    sent(12, gz.at[pl.ds(0, 15)])
    gz[zy] = gsum[zy]

    receive(7)
    hlow[x] = sum_four(hh).astype(BF16)
    x_all(lambda to: hlow.at[x], hlow.at[x], hlow, 9)

    receive(9)
    gradu = (adapter_scale * normalizer_scale) * dot(hlow[...].reshape(ROWS, 128), g_v[...], 0, 0)
    for c in range(2):
        upack[c] = packed_rows(gradu, c, 0)
    rcopy(upack.at[1 - core], ucore, 11, core_peer).start()
    sent(11, ucore)
    receive(11)
    usum[...] = (upack[core].astype(F32) + ucore[...].astype(F32)).astype(BF16)
    zy_all(lambda to: usum.at[to], uz.at[zy], 13)
    sent(13, uz.at[pl.ds(0, 15)])
    uz[zy] = usum[zy]

    for copy in loads[4:]:
        copy.wait()
    receive(12)
    gradient = unpack(jnp.sum(gz[...].astype(F32), axis=0), TD)
    new_p, new_m, new_v = adam(dp_v[...], dm_v[...], dv_v[...], gradient)
    fgat[r, pl.ds(0, PW)] = pack(new_p[:, :WCOLS], TW, PW)
    fgat[r, pl.ds(PW, PW)] = pack(new_p[:, WCOLS:], TW, PW)

    def pass_on(piece, to):
        rcopy(fgat.at[piece], fgat.at[piece], 14, (l, to), roll_sem.at[piece]).start()

    def arrived(j):
        piece = (yhi + j // 4) % 4 * 4 + (x + j % 4) % 4
        if j:
            drain(fgat.at[piece], roll_sem.at[piece])
        return piece

    for j in (2, 1, 3):
        pass_on(r, h_to(j))
    for j in (2, 1, 3):
        pass_on(r, x_to(j))
    leaving.append((14, fgat.at[pl.ds(0, ROLL - 1)]))
    dpo[...] = new_p
    dmo[...] = new_m
    dvo[...] = new_v

    def forward(piece):
        near, far = fgat.at[piece, pl.ds(core * PW, PW)], fgat.at[piece, pl.ds((1 - core) * PW, PW)]
        rcopy(far, fbuf.at[l], 16, (2 * piece + 1 - core, r)).start()

        @pl.when(piece != zy)
        def _():
            rcopy(near, fbuf.at[l], 16, (2 * piece + core, r)).start()

        @pl.when(piece == zy)
        def _():
            pltpu.make_async_copy(near, fbuf.at[l], recv_sem.at[16]).start()

    receive(13)
    gradient = unpack(jnp.sum(uz[...].astype(F32), axis=0), TU)
    new_p, new_m, new_v = adam(up_v[...], um_v[...], uv_v[...], gradient)
    unew[slot] = pack(new_p, TU, PU)
    for dz, dp in ZY_FAR_FIRST:
        for to_core in (core, 1 - core):
            rcopy(unew.at[slot], unew.at[slot], 15, (zy_to(dz, dp) * 2 + to_core, r)).start()
    rcopy(unew.at[slot], unew.at[slot], 15, core_peer).start()
    sent(15, unew.at[pl.ds(0, LEARN - 1)])
    upo[...] = new_p
    umo[...] = new_m
    uvo[...] = new_v

    for j in (0, 1, 3, 2):
        forward(arrived(j))
    for j in (4, 12, 8):
        piece = arrived(j)
        for k in (2, 1, 3):
            pass_on(piece, x_to(k))
        forward(piece)
    for j in (5, 7, 13, 15, 6, 14, 9, 11, 10):
        forward(arrived(j))
    arriving[16] = fbuf
    leaving.append((16, fbuf.at[pl.ds(0, LEARN - 1)]))

    receive(16)
    for k in range(0, TW, 4):
        packed = fbuf[:, OWN * k : OWN * k + 16].reshape(16, 2, 16, 128)
        for t, rows in enumerate(rank_rows((packed[:, 0], packed[:, 1]), min(4, TW - k))):
            dnew[:, 128 * (k + t) : 128 * (k + t) + 128] = rows
    receive(15)
    unpack_up(unew)
    finish()


def merge_kernel(w, umat, dnew, *refs):
    moved, wo_hbm, stored, wo_v, store_sem = refs[:6], refs[6], refs[7:13], refs[13], refs[14]
    stores = []

    def store(src, dst):
        copy = pltpu.make_async_copy(src, dst, store_sem.at[len(stores)])
        copy.start()
        stores.append(copy)

    for src, dst in zip(moved, stored):
        store(src, dst)
    for k in range(4):
        rows = slice(128 * k, 128 * k + 128)
        product = dot(umat[:, rows], dnew[...], 0, 0)
        wo_v[rows] = (w[rows].astype(F32) + adapter_scale * product).astype(BF16)
        store(wo_v.at[rows], wo_hbm.at[rows])
    for copy in stores:
        copy.wait()


def per_device(*args):
    down, up = (OWN, HID), (OWN, OUT)
    small = [down, down, down, up, up, up]
    hbm = pl.BlockSpec(memory_space=pltpu.HBM)
    vmem = pl.BlockSpec(memory_space=pltpu.VMEM)
    dma = pltpu.SemaphoreType.DMA

    def b(*shape):
        return pltpu.VMEM(shape, BF16)

    states = [jax.ShapeDtypeStruct(s, F32) for s in small]
    low = [b(NX, PART, 128) for _ in range(4)]
    made = pl.pallas_call(
        kernel,
        out_shape=[
            jax.ShapeDtypeStruct((OUT, WCOLS), BF16),
            jax.ShapeDtypeStruct((RANK, OUT), BF16),
            jax.ShapeDtypeStruct((RANK, WCOLS), BF16),
        ]
        + states,
        in_specs=[hbm] * 9,
        out_specs=[vmem] * 9,
        scratch_shapes=[b(ROWS, HID), b(ROWS, OUT)]
        + [pltpu.VMEM(s, F32) for s in small]
        + [b(LEARN, PU, 128), b(LEARN, PD, 128), b(RANK, HID)]
        + low
        + low
        + [b(2, 16, PD, 128), b(16, PD, 128), b(16, PD, 128), b(16, PD, 128)]
        + [b(2, 16, PU, 128), b(16, PU, 128), b(16, PU, 128), b(16, PU, 128), b(LEARN, PU, 128)]
        + [b(ROLL, 2 * PW, 128), b(LEARN, PW, 128)]
        + [dma((9,)), dma((18,)), dma((18,)), dma((ROLL,))],
        compiler_params=pltpu.CompilerParams(
            collective_id=0, has_side_effects=True, vmem_limit_bytes=40 * 2**20
        ),
        cost_estimate=pl.CostEstimate(flops=10**9, bytes_accessed=10**7, transcendentals=0),
        name="adapter_step",
    )(*(pltpu.with_memory_space_constraint(a, pltpu.HBM) for a in args))
    return tuple(
        pl.pallas_call(
            merge_kernel,
            out_shape=[jax.ShapeDtypeStruct((OUT, WCOLS), BF16)] + states,
            in_specs=[vmem] * 9,
            out_specs=[hbm] * 7,
            scratch_shapes=[b(OUT, WCOLS), dma((10,))],
            compiler_params=pltpu.CompilerParams(vmem_limit_bytes=20 * 2**20),
            cost_estimate=pl.CostEstimate(flops=10**8, bytes_accessed=2 * 10**6, transcendentals=0),
            name="merge",
        )(*made)
    )


def solution(mesh):
    return jax.shard_map(
        per_device,
        mesh=mesh,
        in_specs=(P("roll", "learn"),) + (P("learn", "roll"),) * 8,
        out_specs=(P("roll", "learn"),) + (P("learn", "roll"),) * 6,
        check_vma=False,
    )
```
